32 devices in a mesh: groups: 2 (over x), ctx: 4 (over y, core), head: 4 (over z).
Axes of the slice: x: 2, y: 2, z: 4, core: 2. Of those that a mesh axis runs over, the one named last changes fastest.
Arguments:
- queries: bfloat16 [256, 16384], P(('groups', 'ctx'), 'head'), parts along dimension 0, may hold values from -8 to 8
- cache_keys: bfloat16 [16384, 1024], P(('groups', 'ctx'), 'head'), parts along dimension 0, may hold values from -6 to 6
- cache_values: bfloat16 [16384, 1024], P(('groups', 'ctx'), 'head'), parts along dimension 0, may hold values from -6 to 6
- new_keys: bfloat16 [256, 1024], P(('groups', 'ctx'), 'head'), parts along dimension 0, may hold values from -8 to 8
- new_values: bfloat16 [256, 1024], P(('groups', 'ctx'), 'head'), parts along dimension 0, may hold values from -6 to 6
- out_weight: bfloat16 [16384, 16384], P('head', 'ctx'), may hold values from -0.1796875 to 0.1796875
- new_counts: int32 [8, 4], P('groups'), parts along dimension 0, may hold values from 1 to 16, 32 in all within a row
- cache_counts: int32 [8, 4], P('groups'), parts along dimension 0, may hold values from 1 to 512, 1536 in all within a row
- row_dest: int32 [256], P('groups'), parts along dimension 0, may hold values from 0 to 127, each once
Outputs:
- projected: bfloat16 [256, 16384], P(('groups', 'head'), 'ctx'), parts along dimension 0
The draws below stay inside these ranges and needn't reach their ends.
There are 2 independent parts, one for each index of `groups`. The reference program is written for one: setup_inputs(seed, part) draws one part's arguments, and reference() takes and returns one part's arrays. A program takes and returns all parts, laid end to end along the dimension named above; an argument that names none is the same for every part. Nothing has to cross between parts.
Inputs may be any that keep to these rules, and one draw needn't show every extreme that they name: Each row of new_counts sums to 32. `cache_counts`: each shard's counts sum to 1536. `row_dest`: each output row is named once.
All inputs are finite; a program needn't handle non-finite values.
Results may differ from the reference program's by a relative error of at most 0.017.
Values may be sent and summed in bfloat16 or wider, within the bound.
No kernel may reach another device: no remote copies, remote signals or barrier semaphores. Data moves between devices by JAX's collectives and lax.ppermute only.
A program may use at most 128 MiB of HBM per device.

```python
import math
import jax
import jax.numpy as jnp
import numpy as np
from jax import lax

D = 16384
HEADS = 128
KV_HEADS = 8
HEAD_DIM = 128
Q_DEV = 32
CACHE_DEV = 2048
RPD = 4
GROUP = 16
TOKENS = 128
REQS = 4
CAPR = 512
N_CTX = 4


def draw_queries(key, part):
    shape = (TOKENS, HEADS * HEAD_DIM)
    base = jnp.clip(jax.random.normal(jax.random.fold_in(key, 21), shape, jnp.float32), -8.0, 8.0)
    return base.astype(jnp.bfloat16)


def draw_new_keys(key, part):
    shape = (TOKENS, KV_HEADS * HEAD_DIM)
    base = jnp.clip(jax.random.normal(jax.random.fold_in(key, 31), shape, jnp.float32), -8.0, 8.0)
    return base.astype(jnp.bfloat16)


def steps_of(rng, dims, pieces, low, high):
    loudness = 1.0
    for dim, blocks in pieces:
        heights = jax.random.uniform(jax.random.fold_in(jax.random.fold_in(rng, 6), dim), (blocks,), jnp.float32, low / len(pieces), high / len(pieces))
        loudness = loudness * jnp.repeat(jnp.exp(heights), dims[dim] // blocks).reshape((-1,) + (1,) * (len(dims) - 1 - dim))
    return loudness


def length_profile(amount, total, reach, lean):
    loads = [(1 << 20) // math.isqrt(rank ** lean) + 1 for rank in range(2, amount + 1)]
    rest, given = total - reach - (amount - 1), [1] * (amount - 1)
    while rest > 0:
        free = [i for i in range(amount - 1) if given[i] < reach]
        pool, budget = sum([loads[i] for i in free]), rest
        for i in free:
            more = min(reach - given[i], max(1, budget * loads[i] // pool), rest)
            given[i] = given[i] + more
            rest = rest - more
    return np.array([reach] + given)


def ragged(stream_key, number_of, total, limit, lean):
    if number_of == 2:
        one = jax.random.randint(stream_key, (), max(1, total - limit), min(limit, total - 1) + 1)
        return jnp.stack([one, total - one])
    tallies = jnp.asarray(length_profile(number_of, total, limit, lean), jnp.int32)
    pairs = (number_of - 1) // 2
    giver, receiver = tallies[1:1 + 2 * pairs:2], tallies[2:2 + 2 * pairs:2]
    margin = jnp.minimum(giver - 1, limit - receiver)
    moved = jax.random.randint(jax.random.fold_in(stream_key, 1), (pairs,), 0, 1 << 20) % (margin + 1)
    tallies = tallies.at[1:1 + 2 * pairs:2].set(giver - moved).at[2:2 + 2 * pairs:2].set(receiver + moved)
    return tallies[jax.random.permutation(jax.random.fold_in(stream_key, 2), number_of)]


def noise(key, dims, scale, limit, pieces=(), held_as=jnp.bfloat16):
    gain = steps_of(key, dims, pieces, -0.22, 0.18) if pieces else 1.0
    array = jax.random.normal(key, dims, jnp.float32) * scale * gain
    return jnp.minimum(jnp.maximum(array, -limit), limit).astype(held_as)


def setup_inputs(seed: int = 0, part: int = 0) -> dict:
    seeds = jax.random.split(jax.random.key(seed), 10)
    own_keys = jax.random.split(jax.random.fold_in(seeds[9], part), 10)
    return {
        "queries": draw_queries(jax.random.fold_in(jax.random.fold_in(seeds[9], part), 71), part),
        "cache_keys": noise(own_keys[1], (N_CTX * CACHE_DEV, KV_HEADS * HEAD_DIM), 1.0, 6.0, ((0, 4), (1, 4))),
        "cache_values": noise(own_keys[2], (N_CTX * CACHE_DEV, KV_HEADS * HEAD_DIM), 1.0, 6.0, ((0, 4), (1, 4))),
        "new_keys": draw_new_keys(jax.random.fold_in(jax.random.fold_in(seeds[9], part), 71), part),
        "new_values": noise(own_keys[4], (TOKENS, KV_HEADS * HEAD_DIM), 1.0, 6.0, ((0, 4), (1, 4))),
        "out_weight": noise(seeds[5], (HEADS * HEAD_DIM, D), 0.03, 0.1796875, ((0, 4), (1, 4))),
        "new_counts": jax.vmap(lambda own: ragged(own, RPD, Q_DEV, Q_DEV // 2, 2))(jax.random.split(own_keys[6], N_CTX)).reshape((N_CTX, RPD)).astype(jnp.int32),
        "cache_counts": jax.vmap(lambda own: ragged(own, REQS, CACHE_DEV * 3 // 4, CAPR, 2))(jax.random.split(own_keys[7], N_CTX)).reshape((N_CTX, REQS)).astype(jnp.int32),
        "row_dest": jax.random.permutation(own_keys[8], TOKENS).astype(jnp.int32),
    }


NEG = -1e+30

def row_requests(new_counts):
    ends = jnp.cumsum(new_counts, axis=1).astype(jnp.int32)
    offsets = jnp.arange(Q_DEV, dtype=jnp.int32)
    inside = lax.optimization_barrier(jnp.sum((offsets[None, :, None] >= ends[:, None, :]).astype(jnp.int32), axis=2))
    return inside.reshape(-1).astype(jnp.int32)

def cache_requests(cache_counts):
    ends = jnp.cumsum(cache_counts, axis=1).astype(jnp.int32)
    offsets = jnp.arange(CACHE_DEV, dtype=jnp.int32)
    return lax.optimization_barrier(jnp.sum((offsets[None, :, None] >= ends[:, None, :]).astype(jnp.int32), axis=2)).astype(jnp.int32)

def shard_partial(queries, query_req, query_pos, keys, values, key_req, key_pos):
    count = queries.shape[0]
    width = keys.shape[0]
    q_heads = queries.astype(jnp.float32).reshape(count, KV_HEADS, GROUP, HEAD_DIM)
    k_heads = keys.astype(jnp.float32).reshape(width, KV_HEADS, HEAD_DIM)
    v_heads = values.astype(jnp.float32).reshape(width, KV_HEADS, HEAD_DIM)
    scores = jnp.einsum('nhgd,khd->hngk', q_heads, k_heads) * (1.0 / math.sqrt(HEAD_DIM))
    visible = (key_req[None, :] == query_req[:, None]) & (key_pos[None, :] <= query_pos[:, None])
    visible = visible[None, :, None, :]
    top = lax.optimization_barrier(jnp.max(jnp.where(visible, scores, NEG), axis=3))
    probs = jnp.where(visible, jnp.exp(scores - top[..., None]), 0.0).astype(jnp.bfloat16)
    total = lax.optimization_barrier(jnp.sum(probs.astype(jnp.float32), axis=3))
    mixed = jnp.einsum('hngk,khd->nhgd', probs.astype(jnp.float32), v_heads)
    scale = jnp.maximum(total, 1.0).transpose(1, 0, 2)
    partial_value = (mixed / scale[..., None]).astype(jnp.bfloat16).reshape(count, -1)
    return (partial_value, top.transpose(1, 0, 2).reshape(count, -1), total.transpose(1, 0, 2).reshape(count, -1))

def reference(queries, cache_keys, cache_values, new_keys, new_values, out_weight, new_counts, cache_counts, row_dest):
    row_req = row_requests(new_counts)
    cache_req = cache_requests(cache_counts)
    positions = jnp.arange(TOKENS, dtype=jnp.int32)
    marks = jnp.full((CACHE_DEV,), -1, dtype=jnp.int32)

    def one_shard(items):
        shard_keys, shard_values, shard_req, fresh_keys, fresh_values, fresh_req, fresh_pos = items
        keys = jnp.concatenate([shard_keys, fresh_keys], axis=0)
        values = jnp.concatenate([shard_values, fresh_values], axis=0)
        key_req = jnp.concatenate([shard_req, fresh_req], axis=0).astype(jnp.int32)
        key_pos = jnp.concatenate([marks, fresh_pos], axis=0).astype(jnp.int32)
        return shard_partial(queries, row_req, positions, keys, values, key_req, key_pos)
    items = (cache_keys.reshape(N_CTX, CACHE_DEV, -1), cache_values.reshape(N_CTX, CACHE_DEV, -1), cache_req, new_keys.reshape(N_CTX, Q_DEV, -1), new_values.reshape(N_CTX, Q_DEV, -1), row_req.reshape(N_CTX, Q_DEV), positions.reshape(N_CTX, Q_DEV))
    partials, tops, totals = lax.map(one_shard, items)
    best = lax.optimization_barrier(jnp.max(tops, axis=0))
    weights = jnp.exp(tops - best[None]) * totals
    numer = lax.optimization_barrier(jnp.sum(weights[..., None] * partials.reshape(N_CTX, TOKENS, HEADS, HEAD_DIM).astype(jnp.float32), axis=0))
    attention = (numer / lax.optimization_barrier(jnp.sum(weights, axis=0))[..., None]).astype(jnp.bfloat16).reshape(TOKENS, -1)
    ordered = jnp.zeros_like(attention).at[row_dest].set(attention)
    return jnp.dot(ordered, out_weight, preferred_element_type=jnp.float32).astype(jnp.bfloat16)
```

```python
import functools
import math

import jax
import jax.numpy as jnp
from jax import lax
from jax.experimental import pallas as pl
from jax.experimental.pallas import tpu as pltpu
from jax.sharding import PartitionSpec as P

HEAD_DIM = 128
CAPR = 512
ROWS = 16
ALIGN = 16
NEG = -1e30
SCALE = 1.0 / math.sqrt(HEAD_DIM)
LOG2E = math.log2(math.e)


def attention_kernel(
    blocks, shards, reqs, pieces, window,
    place, new_counts, cache_counts,
    pos_ref, dest_ref, t_ref, *rest,
):
    q_refs = rest[:pieces]
    k_refs = rest[pieces : pieces + shards]
    v_refs = rest[pieces + shards : pieces + 2 * shards]
    nk_refs = rest[pieces + 2 * shards : pieces + 3 * shards]
    nv_refs = rest[pieces + 3 * shards : pieces + 4 * shards]
    out_ref, stat_ref, sorted_q, part, stat = rest[pieces + 4 * shards :]
    padded = sorted_q.shape[0]
    cols = sorted_q.shape[1]
    group = cols // HEAD_DIM
    all_rows = out_ref.shape[0]
    block_rows = nk_refs[0].shape[0]
    shard_rows = k_refs[0].shape[0]
    me = place[0]

    sorter = (
        lax.broadcasted_iota(jnp.int32, (padded, all_rows), 0) == pos_ref[...]
    ).astype(jnp.bfloat16)
    rows_in = jnp.concatenate([q[...] for q in q_refs], axis=0)
    sorted_q[...] = jnp.dot(sorter, rows_in, preferred_element_type=jnp.float32).astype(
        jnp.bfloat16
    )
    part[...] = jnp.zeros_like(part)
    stat[...] = jnp.zeros_like(stat)

    ends = []
    last = jnp.int32(0)
    for r in range(reqs):
        amount = new_counts[0, r]
        for b in range(1, blocks):
            amount = amount + new_counts[b, r]
        last = last + (amount + (ROWS - 1)) // ROWS
        ends.append(last)

    width = shards * (window + block_rows)
    plain = (shards * window) // 128 * 128
    key = lax.broadcasted_iota(jnp.int32, (1, width), 1)
    lane = lax.broadcasted_iota(jnp.int32, (ROWS, 128), 1)
    ones = jnp.ones((width, HEAD_DIM), jnp.bfloat16)

    def tile(i, carry):
        r = jnp.int32(0)
        for e in ends[:-1]:
            r = r + (i >= e).astype(jnp.int32)
        inside = None
        key_pos = jnp.full((1, width), -1, jnp.int32)
        ks, vs = [], []
        for j in range(shards):
            shard = place[1 + j]
            low = jnp.int32(0)
            new_low = jnp.int32(0)
            for o in range(reqs - 1):
                low = low + jnp.where(o < r, cache_counts[shard, o], 0)
                new_low = new_low + jnp.where(o < r, new_counts[shard, o], 0)
            high = low + cache_counts[shard, r]
            new_high = new_low + new_counts[shard, r]
            start = jnp.clip(low // ALIGN * ALIGN, 0, shard_rows - window)
            start = pl.multiple_of(start, ALIGN)
            ks.append(k_refs[j][pl.ds(start, window), :])
            vs.append(v_refs[j][pl.ds(start, window), :])
            first = key - j * window + start
            seen = (key >= j * window) & (key < (j + 1) * window)
            seen = seen & (first >= low) & (first < high)
            inside = seen if inside is None else inside | seen
            base = shards * window + j * block_rows
            fresh = key - base
            seen = (key >= base) & (fresh < block_rows)
            key_pos = jnp.where(seen, shard * block_rows + fresh, key_pos)
            inside = inside | (seen & (fresh >= new_low) & (fresh < new_high))
        ks = jnp.concatenate(ks + [k[...] for k in nk_refs], axis=0)
        vs = jnp.concatenate(vs + [v[...] for v in nv_refs], axis=0)
        row0 = pl.multiple_of(i * ROWS, ROWS)
        q = jnp.concatenate(
            [
                sorted_q[pl.ds(row0, ROWS), g * HEAD_DIM : (g + 1) * HEAD_DIM]
                for g in range(group)
            ],
            axis=0,
        )
        scores = lax.dot_general(
            q, ks, (((1,), (1,)), ((), ())), preferred_element_type=jnp.float32
        )
        bias = jnp.where(inside, 0.0, NEG)
        t = t_ref[pl.ds(row0, ROWS), :]
        causal = jnp.where(key_pos[:, plain:] <= t, bias[:, plain:], NEG)
        causal = jnp.concatenate([causal] * group, axis=0)
        scores = jnp.concatenate(
            [scores[:, :plain] + bias[:, :plain], scores[:, plain:] + causal], axis=1
        )
        top = jnp.max(scores, axis=1, keepdims=True)
        probs = jnp.exp2((scores - top) * (SCALE * LOG2E)).astype(jnp.bfloat16)
        mixed = jnp.dot(
            probs,
            jnp.concatenate([vs, ones], axis=1),
            preferred_element_type=jnp.float32,
        )
        total = mixed[:, HEAD_DIM:]
        value = (mixed[:, :HEAD_DIM] / total).astype(jnp.bfloat16)
        lse = top * SCALE + jnp.log(total)
        packed = jnp.zeros((ROWS, 128), jnp.float32)
        for g in range(group):
            rows = slice(g * ROWS, (g + 1) * ROWS)
            part[pl.ds(row0, ROWS), g * HEAD_DIM : (g + 1) * HEAD_DIM] = value[rows]
            packed = jnp.where(lane == g, lse[rows], packed)
        stat[pl.ds(row0, ROWS), :] = packed
        return carry

    lax.fori_loop(0, last, tile, jnp.int32(0))

    landing = (
        lax.broadcasted_iota(jnp.int32, (all_rows, all_rows), 0) == dest_ref[...]
    ).astype(jnp.bfloat16)
    router = lax.dot_general(
        landing, sorter, (((1,), (1,)), ((), ())), preferred_element_type=jnp.float32
    )
    out_ref[...] = jnp.dot(
        router.astype(jnp.bfloat16), part[...], preferred_element_type=jnp.float32
    ).astype(jnp.bfloat16)
    stat_ref[...] = jnp.dot(
        router,
        stat[...],
        precision=lax.Precision.HIGHEST,
        preferred_element_type=jnp.float32,
    )


def attend(place, new_counts, cache_counts, pos, dest, t_sorted, q, k, v, nk, nv, own, kv):
    blocks, reqs = new_counts.shape
    all_rows = pos.shape[1]
    padded = t_sorted.shape[0]
    shards = len(k)
    cols = q[0].shape[1] // own // kv
    shard_rows = k[0].shape[0]
    window = min(CAPR + ALIGN, shard_rows)

    def columns(arrays, width):
        specs = []
        for number, a in enumerate(arrays):
            if number == 0 and own > 1:
                index = lambda i, p, *_: (0, p[3] * kv + i)
            else:
                index = lambda i, *_: (0, i)
            specs.append(pl.BlockSpec((a.shape[0], width), index))
        return specs

    whole = lambda a: pl.BlockSpec(a.shape, lambda i, *_: (0, 0))
    return pl.pallas_call(
        functools.partial(attention_kernel, blocks, shards, reqs, len(q), window),
        grid_spec=pltpu.PrefetchScalarGridSpec(
            num_scalar_prefetch=3,
            grid=(kv,),
            in_specs=[whole(pos), whole(dest), whole(t_sorted)]
            + columns(q, cols)
            + columns(k, HEAD_DIM)
            + columns(v, HEAD_DIM)
            + columns(nk, HEAD_DIM)
            + columns(nv, HEAD_DIM),
            out_specs=[
                pl.BlockSpec((all_rows, cols), lambda i, *_: (0, i)),
                pl.BlockSpec((all_rows, 128), lambda i, *_: (0, i)),
            ],
            scratch_shapes=[
                pltpu.VMEM((padded, cols), jnp.bfloat16),
                pltpu.VMEM((padded, cols), jnp.bfloat16),
                pltpu.VMEM((padded, 128), jnp.float32),
            ],
        ),
        out_shape=[
            jax.ShapeDtypeStruct((all_rows, cols * kv), jnp.bfloat16),
            jax.ShapeDtypeStruct((all_rows, 128 * kv), jnp.float32),
        ],
        compiler_params=pltpu.CompilerParams(vmem_limit_bytes=24 * 2**20),
        name="attend",
    )(place, new_counts, cache_counts, pos, dest, t_sorted, *q, *k, *v, *nk, *nv)


def combine_kernel(group, a_ref, b_ref, sa_ref, sb_ref, out_ref):
    sa, sb = sa_ref[...], sb_ref[...]
    best = jnp.maximum(sa, sb)
    wa, wb = jnp.exp(sa - best), jnp.exp(sb - best)
    whole = wa + wb
    wa, wb = wa / whole, wb / whole
    for g in range(group):
        at = slice(g * HEAD_DIM, (g + 1) * HEAD_DIM)
        mixed = wa[:, g : g + 1] * a_ref[:, at].astype(jnp.float32)
        mixed = mixed + wb[:, g : g + 1] * b_ref[:, at].astype(jnp.float32)
        out_ref[:, at] = mixed.astype(jnp.bfloat16)


def combine_two(a, b, sa, sb, kv):
    rows, cols = a.shape
    cols = cols // kv
    spec = pl.BlockSpec((rows, cols), lambda i: (0, i))
    stat = pl.BlockSpec((rows, 128), lambda i: (0, i))
    return pl.pallas_call(
        functools.partial(combine_kernel, cols // HEAD_DIM),
        grid=(kv,),
        in_specs=[spec, spec, stat, stat],
        out_specs=spec,
        out_shape=jax.ShapeDtypeStruct(a.shape, jnp.bfloat16),
        compiler_params=pltpu.CompilerParams(vmem_limit_bytes=24 * 2**20),
        name="combine",
    )(a, b, sa, sb)


def project_kernel(parts, heads, order, *refs):
    a_refs, w_refs, outs = refs[:parts], refs[parts : 2 * parts], refs[2 * parts :]
    total = jnp.dot(a_refs[0][...], w_refs[0][...], preferred_element_type=jnp.float32)
    for a, w in zip(a_refs[1:], w_refs[1:]):
        total = total + jnp.dot(a[...], w[...], preferred_element_type=jnp.float32)
    rows = total.shape[0] // heads
    for d, out in enumerate(outs):
        out[...] = total[d * rows : (d + 1) * rows].astype(out.dtype)


def project(order, parts, weight, heads):
    rows = parts[0].shape[0]
    depth, width = weight.shape
    depth = depth // len(parts)
    step = min(512, width)
    weights = [
        pl.BlockSpec((depth, step), lambda j, o, n=n: (o[n], j)) for n in range(len(parts))
    ]
    return pl.pallas_call(
        functools.partial(project_kernel, len(parts), heads),
        grid_spec=pltpu.PrefetchScalarGridSpec(
            num_scalar_prefetch=1,
            grid=(width // step,),
            in_specs=[pl.BlockSpec(a.shape, lambda j, o: (0, 0)) for a in parts] + weights,
            out_specs=[pl.BlockSpec((rows // heads, step), lambda j, o: (0, j))] * heads,
        ),
        out_shape=[
            jax.ShapeDtypeStruct((rows // heads, width), jnp.float32 if d == 0 else jnp.bfloat16)
            for d in range(heads)
        ],
        compiler_params=pltpu.CompilerParams(vmem_limit_bytes=40 * 2**20),
        name="project",
    )(order, *parts, *([weight] * len(parts)))


def per_device(
    queries,
    cache_keys,
    cache_values,
    new_keys,
    new_values,
    out_weight,
    new_counts,
    cache_counts,
    row_dest,
):
    blocks = lax.axis_size("ctx")
    heads = lax.axis_size("head")
    me = lax.axis_index("ctx")
    my_head = lax.axis_index("head")
    block_rows = queries.shape[0]
    all_rows = block_rows * blocks
    reqs = new_counts.shape[1]
    kv_here = cache_keys.shape[1] // HEAD_DIM
    paired = blocks == 4 and kv_here % 2 == 0
    half = me % 2
    even = heads & (heads - 1) == 0

    if paired:
        near = [(i, i ^ 1) for i in range(blocks)]
        far = [(i, i ^ 2) for i in range(blocks)]
        across = [(i, i ^ 3) for i in range(blocks)]

        def part_of(a, which):
            width = a.shape[1] // 2
            return lax.dynamic_slice_in_dim(a, which * width, width, axis=1)

        q_mine, q_other = part_of(queries, half), part_of(queries, 1 - half)
        q_far = lax.ppermute(q_mine, "ctx", far)
        q_across = lax.ppermute(q_other, "ctx", across)
        q_near = lax.ppermute(q_other, "ctx", near)
        sets = [
            [a, lax.ppermute(part_of(a, 1 - half), "ctx", near)]
            for a in (cache_keys, cache_values, new_keys, new_values)
        ]
        pieces = [queries, q_near, q_far, q_across]
        piece_block = me ^ jnp.arange(blocks, dtype=jnp.int32)
        place = jnp.stack([me, me, me ^ 1, half]).astype(jnp.int32)
        own, kv = 2, kv_here // 2
    else:
        pieces = [lax.all_gather(queries, "ctx", axis=0, tiled=True)]
        sets = [[a] for a in (cache_keys, cache_values, new_keys, new_values)]
        piece_block = jnp.arange(blocks, dtype=jnp.int32)
        place = jnp.stack([me, me, me, half]).astype(jnp.int32)
        own, kv = 1, kv_here

    pick = (piece_block[:, None] == jnp.arange(blocks, dtype=jnp.int32)[None, :]).astype(jnp.int32)
    counts = jnp.sum(pick[:, :, None] * new_counts[None], axis=1)
    dest = jnp.sum(pick[:, :, None] * row_dest.reshape(1, blocks, block_rows), axis=1).reshape(-1)
    lower = jnp.tril(jnp.ones((reqs, reqs), jnp.int32))
    ends = jnp.sum(counts[:, None, :] * lower[None], axis=2)
    offsets = jnp.arange(block_rows, dtype=jnp.int32)
    req = jnp.sum((offsets[None, :, None] >= ends[:, None, :]).astype(jnp.int32), axis=2).reshape(-1)
    row = (piece_block[:, None] * block_rows + offsets[None, :]).reshape(-1)
    amounts = jnp.sum(new_counts, axis=0)
    tiles = (amounts + (ROWS - 1)) // ROWS
    before = (req[None, :] == req[:, None]) & (row[None, :] < row[:, None])
    pos = jnp.sum(before.astype(jnp.int32), axis=1) + ROWS * jnp.sum(
        tiles[None, :] * (jnp.arange(reqs)[None, :] < req[:, None]), axis=1
    )
    padded = (all_rows + reqs * (ROWS - 1)) // ROWS * ROWS
    t_sorted = jnp.sum(
        jnp.where(pos[None, :] == jnp.arange(padded)[:, None], row[None, :], 0), axis=1, keepdims=True
    )
    out_rows = all_rows // heads
    dest_head = dest // out_rows
    dest_head = dest_head ^ my_head if even else (dest_head - my_head) % heads
    dest = dest_head * out_rows + dest % out_rows

    part, stat = attend(
        place, new_counts, cache_counts, pos[None, :], dest[None, :], t_sorted, pieces, *sets, own, kv
    )

    if paired:
        part_far = lax.ppermute(part, "ctx", far)
        stat_far = lax.ppermute(stat, "ctx", far)
        mine = combine_two(part, part_far, stat, stat_far, kv)
        sums = [mine, lax.ppermute(mine, "ctx", near)]
        order = jnp.stack([half, 1 - half]).astype(jnp.int32)
    else:
        group = part.shape[1] // HEAD_DIM // kv
        got = lax.all_to_all(part.reshape(blocks, block_rows, -1), "ctx", 0, 0, tiled=True)
        logs = lax.all_to_all(stat.reshape(blocks, block_rows, -1), "ctx", 0, 0, tiled=True)
        logs = logs.reshape(blocks, block_rows, kv, 128)[..., :group]
        weights = jnp.exp(logs - jnp.max(logs, axis=0)[None])
        weights = weights / jnp.sum(weights, axis=0)[None]
        stacked = got.reshape(blocks, block_rows, kv, group, HEAD_DIM).astype(jnp.float32)
        mine = jnp.sum(weights[..., None] * stacked, axis=0).astype(jnp.bfloat16)
        sums = [lax.all_gather(mine.reshape(block_rows, -1), "ctx", axis=0, tiled=True)]
        order = jnp.zeros((1,), jnp.int32)

    shares = project(order, sums, out_weight, heads)
    total = shares[0]
    for d in range(1, heads):
        perm = [(i, i ^ d if even else (i + d) % heads) for i in range(heads)]
        total = total + lax.ppermute(shares[d], "head", perm).astype(jnp.float32)
    return total.astype(jnp.bfloat16)


def solution(mesh):
    return jax.shard_map(
        per_device,
        mesh=mesh,
        in_specs=(
            P(("groups", "ctx"), "head"),
            P(("groups", "ctx"), "head"),
            P(("groups", "ctx"), "head"),
            P(("groups", "ctx"), "head"),
            P(("groups", "ctx"), "head"),
            P("head", "ctx"),
            P("groups", None),
            P("groups", None),
            P("groups"),
        ),
        out_specs=P(("groups", "head"), "ctx"),
        check_vma=False,
    )
```

```python
import functools
import math

import jax
import jax.numpy as jnp
from jax import lax
from jax.experimental import pallas as pl
from jax.experimental.pallas import tpu as pltpu
from jax.sharding import PartitionSpec as P

HEAD_DIM = 128
CAPR = 512
ROWS = 16
ALIGN = 16
NEG = -1e30
SCALE = 1.0 / math.sqrt(HEAD_DIM)
LOG2E = math.log2(math.e)


def in_hbm(a):
    return pltpu.with_memory_space_constraint(a, pltpu.HBM)


def pack_kernel(number, kv, index, *refs):
    sources, out_ref, sems = refs[:-2], refs[-2], refs[-1]
    block = index[0] * kv + number
    copies = []
    at = 0
    for ref in sources[:4]:
        rows = ref.shape[0]
        columns = pl.ds(pl.multiple_of(block * HEAD_DIM, HEAD_DIM), HEAD_DIM)
        copies.append((ref.at[:, columns], out_ref.at[at : at + rows, :]))
        at += rows
    for ref in sources[4:]:
        rows = ref.shape[0]
        heads = (out_ref.shape[0] - at) // rows
        for g in range(heads):
            columns = pl.ds(pl.multiple_of((block * heads + g) * HEAD_DIM, HEAD_DIM), HEAD_DIM)
            copies.append((ref.at[:, columns], out_ref.at[at : at + rows, :]))
            at += rows
    copies = [pltpu.make_async_copy(a, b, sems.at[n]) for n, (a, b) in enumerate(copies)]
    for c in copies:
        c.start()
    for c in copies:
        c.wait()


def pack(index, arrays, queries, kv, number):
    group = queries[0].shape[1] // arrays[0].shape[1] if queries else 0
    rows = sum(a.shape[0] for a in arrays) + sum(q.shape[0] * group for q in queries)
    return pl.pallas_call(
        functools.partial(pack_kernel, number, kv),
        in_specs=[pl.BlockSpec(memory_space=pltpu.SMEM)]
        + [pl.BlockSpec(memory_space=pltpu.HBM)] * (len(arrays) + len(queries)),
        out_specs=pl.BlockSpec(memory_space=pltpu.VMEM),
        out_shape=jax.ShapeDtypeStruct((rows, HEAD_DIM), arrays[0].dtype),
        scratch_shapes=[pltpu.SemaphoreType.DMA((len(arrays) + group,))],
        compiler_params=pltpu.CompilerParams(vmem_limit_bytes=4 * 2**20),
        name="pack",
    )(index.reshape(1), *[in_hbm(a) for a in (*arrays, *queries)])


def split_kernel(index, q_ref, *refs):
    outs, sems = refs[:-1], refs[-1]
    width = outs[0].shape[1]
    copies = []
    for n, out in enumerate(outs):
        columns = pl.ds(pl.multiple_of((index[0] ^ n) * width, width), width)
        copies.append(pltpu.make_async_copy(q_ref.at[:, columns], out, sems.at[n]))
    for c in copies:
        c.start()
    for c in copies:
        c.wait()


def split(index, a):
    half = jax.ShapeDtypeStruct((a.shape[0], a.shape[1] // 2), a.dtype)
    return pl.pallas_call(
        split_kernel,
        in_specs=[pl.BlockSpec(memory_space=pltpu.SMEM), pl.BlockSpec(memory_space=pltpu.HBM)],
        out_specs=[pl.BlockSpec(memory_space=pltpu.VMEM)] * 2,
        out_shape=[half, half],
        scratch_shapes=[pltpu.SemaphoreType.DMA((2,))],
        compiler_params=pltpu.CompilerParams(vmem_limit_bytes=2 * 2**20),
        name="split",
    )(index.reshape(1), in_hbm(a))


def attention_kernel(
    blocks, sets, query_blocks, reqs, window, shard_rows, block_rows, near_queries,
    numbers, *rest,
):
    packed = rest[:sets]
    q_refs = rest[sets:-5]
    out_ref, stat_ref, sorted_q, part, stat = rest[-5:]
    shards = sets
    padded = sorted_q.shape[0]
    cols = sorted_q.shape[1]
    group = cols // HEAD_DIM
    all_rows = out_ref.shape[0]
    base_new = sets + query_blocks
    base_cache = base_new + blocks * reqs

    def new_counts(b, r):
        return numbers[base_new + b * reqs + r]

    def cache_counts(b, r):
        return numbers[base_cache + b * reqs + r]

    row_blocks = [numbers[sets + b] for b in range(query_blocks)]
    starts = [[jnp.int32(0)] for _ in row_blocks]
    bases = [[] for _ in row_blocks]
    tile_ends = []
    last = jnp.int32(0)
    for r in range(reqs):
        amount = jnp.int32(0)
        for b, block in enumerate(row_blocks):
            bases[b].append(amount)
            amount = amount + new_counts(block, r)
            starts[b].append(starts[b][-1] + new_counts(block, r))
        last = last + (amount + (ROWS - 1)) // ROWS
        tile_ends.append(last)
    tile_starts = [jnp.int32(0)] + tile_ends[:-1]

    offset = lax.broadcasted_iota(jnp.int32, (1, all_rows), 1)
    pos = jnp.zeros((1, all_rows), jnp.int32)
    for b in range(query_blocks):
        here = offset - b * block_rows
        for r in range(reqs):
            mine = (here >= starts[b][r]) & (here < starts[b][r + 1])
            mine = mine & (here >= 0) & (here < block_rows)
            first = tile_starts[r] * ROWS + bases[b][r] - starts[b][r]
            pos = jnp.where(mine, first + here, pos)
    sorter = (lax.broadcasted_iota(jnp.int32, (padded, all_rows), 0) == pos).astype(jnp.bfloat16)
    rows_in = [q[...] for q in q_refs]
    if near_queries:
        first = 2 * (shard_rows + block_rows)
        near = [
            packed[1][first + g * block_rows : first + (g + 1) * block_rows, :]
            for g in range(group)
        ]
        rows_in.insert(1, jnp.concatenate(near, axis=1))
    rows_in = jnp.concatenate(rows_in, axis=0)
    sorted_q[...] = jnp.dot(sorter, rows_in, preferred_element_type=jnp.float32).astype(
        jnp.bfloat16
    )
    part[...] = jnp.zeros_like(part)
    stat[...] = jnp.zeros_like(stat)

    width = shards * (window + block_rows)
    plain = (shards * window) // 128 * 128
    key = lax.broadcasted_iota(jnp.int32, (1, width), 1)
    lane = lax.broadcasted_iota(jnp.int32, (ROWS, 128), 1)
    ones = jnp.ones((width, HEAD_DIM), jnp.bfloat16)

    def tile(i, carry):
        r = jnp.int32(0)
        start_tile = jnp.int32(0)
        for e in tile_ends[:-1]:
            r = r + (i >= e).astype(jnp.int32)
            start_tile = jnp.where(i >= e, e, start_tile)
        inside = None
        key_pos = jnp.full((1, width), -1, jnp.int32)
        ks, vs = [], []
        for j in range(shards):
            shard = numbers[j]
            low = jnp.int32(0)
            new_low = jnp.int32(0)
            for o in range(reqs - 1):
                low = low + jnp.where(o < r, cache_counts(shard, o), 0)
                new_low = new_low + jnp.where(o < r, new_counts(shard, o), 0)
            high = low + cache_counts(shard, r)
            new_high = new_low + new_counts(shard, r)
            start = jnp.clip(low // ALIGN * ALIGN, 0, shard_rows - window)
            start = pl.multiple_of(start, ALIGN)
            ks.append(packed[j][pl.ds(start, window), :])
            vs.append(packed[j][pl.ds(pl.multiple_of(start + shard_rows, ALIGN), window), :])
            first = key - j * window + start
            seen = (key >= j * window) & (key < (j + 1) * window)
            seen = seen & (first >= low) & (first < high)
            inside = seen if inside is None else inside | seen
            base = shards * window + j * block_rows
            fresh = key - base
            seen = (key >= base) & (fresh < block_rows)
            key_pos = jnp.where(seen, shard * block_rows + fresh, key_pos)
            inside = inside | (seen & (fresh >= new_low) & (fresh < new_high))
        after = 2 * shard_rows
        for j in range(shards):
            ks.append(packed[j][after : after + block_rows, :])
            vs.append(packed[j][after + block_rows : after + 2 * block_rows, :])
        ks = jnp.concatenate(ks, axis=0)
        vs = jnp.concatenate(vs, axis=0)
        row0 = pl.multiple_of(i * ROWS, ROWS)
        q = jnp.concatenate(
            [
                sorted_q[pl.ds(row0, ROWS), g * HEAD_DIM : (g + 1) * HEAD_DIM]
                for g in range(group)
            ],
            axis=0,
        )
        scores = lax.dot_general(
            q, ks, (((1,), (1,)), ((), ())), preferred_element_type=jnp.float32
        )
        bias = jnp.where(inside, 0.0, NEG)
        t = jnp.zeros((ROWS, 1), jnp.int32)
        among = (i - start_tile) * ROWS + lax.broadcasted_iota(jnp.int32, (ROWS, 1), 0)
        base = jnp.int32(0)
        for block in row_blocks:
            begin = jnp.int32(0)
            for o in range(reqs - 1):
                begin = begin + jnp.where(o < r, new_counts(block, o), 0)
            t = jnp.where(among >= base, block * block_rows + begin + among - base, t)
            base = base + new_counts(block, r)
        causal = jnp.where(key_pos[:, plain:] <= t, bias[:, plain:], NEG)
        causal = jnp.concatenate([causal] * group, axis=0)
        scores = jnp.concatenate(
            [scores[:, :plain] + bias[:, :plain], scores[:, plain:] + causal], axis=1
        )
        top = jnp.max(scores, axis=1, keepdims=True)
        probs = jnp.exp2((scores - top) * (SCALE * LOG2E)).astype(jnp.bfloat16)
        mixed = jnp.dot(
            probs,
            jnp.concatenate([vs, ones], axis=1),
            preferred_element_type=jnp.float32,
        )
        total = mixed[:, HEAD_DIM:]
        value = (mixed[:, :HEAD_DIM] / total).astype(jnp.bfloat16)
        lse = top * SCALE + jnp.log(total)
        logs = jnp.zeros((ROWS, 128), jnp.float32)
        for g in range(group):
            rows = slice(g * ROWS, (g + 1) * ROWS)
            part[pl.ds(row0, ROWS), g * HEAD_DIM : (g + 1) * HEAD_DIM] = value[rows]
            logs = jnp.where(lane == g, lse[rows], logs)
        stat[pl.ds(row0, ROWS), :] = logs
        return carry

    lax.fori_loop(0, last, tile, jnp.int32(0))

    back = (((0,), (0,)), ((), ()))
    out_ref[...] = lax.dot_general(
        sorter, part[...], back, preferred_element_type=jnp.float32
    ).astype(jnp.bfloat16)
    stat_ref[...] = lax.dot_general(
        sorter.astype(jnp.float32),
        stat[...],
        back,
        precision=lax.Precision.HIGHEST,
        preferred_element_type=jnp.float32,
    )


def attend(numbers, packed, queries, cols, number, sizes, query_blocks, near_queries):
    blocks, reqs, shard_rows, block_rows = sizes
    all_rows = query_blocks * block_rows
    padded = (all_rows + reqs * (ROWS - 1)) // ROWS * ROWS
    sets = len(packed)
    window = min(CAPR + ALIGN, shard_rows)
    vmem = pl.BlockSpec(memory_space=pltpu.VMEM)
    return pl.pallas_call(
        functools.partial(
            attention_kernel,
            blocks, sets, query_blocks, reqs, window, shard_rows, block_rows, near_queries,
        ),
        grid_spec=pltpu.PrefetchScalarGridSpec(
            num_scalar_prefetch=1,
            grid=(1,),
            in_specs=[vmem] * sets
            + [pl.BlockSpec((a.shape[0], cols), lambda i, p: (0, number)) for a in queries],
            out_specs=[vmem, vmem],
            scratch_shapes=[
                pltpu.VMEM((padded, cols), jnp.bfloat16),
                pltpu.VMEM((padded, cols), jnp.bfloat16),
                pltpu.VMEM((padded, 128), jnp.float32),
            ],
        ),
        out_shape=[
            jax.ShapeDtypeStruct((all_rows, cols), jnp.bfloat16),
            jax.ShapeDtypeStruct((all_rows, 128), jnp.float32),
        ],
        compiler_params=pltpu.CompilerParams(vmem_limit_bytes=12 * 2**20),
        cost_estimate=pl.CostEstimate(
            flops=8 * padded * cols * sets * window,
            bytes_accessed=16 * 2**20,
            transcendentals=0,
        ),
        name="attend",
    )(numbers, *packed, *queries)


def combine_kernel(group, dest_ref, *refs):
    out_ref = refs[-1]
    rows = out_ref.shape[0]
    landing = (lax.broadcasted_iota(jnp.int32, (rows, rows), 0) == dest_ref[...]).astype(jnp.bfloat16)
    weights = []
    for n in range(0, len(refs) - 1, 4):
        sa, sb = refs[n + 2][...], refs[n + 3][...]
        best = jnp.maximum(sa, sb)
        wa, wb = jnp.exp(sa - best), jnp.exp(sb - best)
        whole = wa + wb
        weights.append((wa / whole, wb / whole))
    for g in range(group):
        at = slice(g * HEAD_DIM, (g + 1) * HEAD_DIM)
        mixed = []
        for n, (wa, wb) in enumerate(weights):
            one = wa[:, g : g + 1] * refs[4 * n][:, at].astype(jnp.float32)
            one = one + wb[:, g : g + 1] * refs[4 * n + 1][:, at].astype(jnp.float32)
            mixed.append(one.astype(jnp.bfloat16))
        mixed = jnp.concatenate(mixed, axis=0)
        out_ref[:, at] = jnp.dot(landing, mixed, preferred_element_type=jnp.float32).astype(jnp.bfloat16)


def combine(dest, phases):
    vmem = pl.BlockSpec(memory_space=pltpu.VMEM)
    arrays = [a for phase in phases for a in phase]
    cols = arrays[0].shape[1]
    return pl.pallas_call(
        functools.partial(combine_kernel, cols // HEAD_DIM),
        in_specs=[vmem] * (1 + len(arrays)),
        out_specs=vmem,
        out_shape=jax.ShapeDtypeStruct((dest.shape[1], cols), jnp.bfloat16),
        compiler_params=pltpu.CompilerParams(vmem_limit_bytes=8 * 2**20),
        name="combine",
    )(dest, *arrays)


def project_kernel(parts, added, cuts, first, step, order, *refs):
    a_refs, w_ref = refs[:parts], refs[parts]
    rest = refs[parts + 1 :]
    total_refs, outs = rest[:added], rest[added : added + len(cuts)]
    held, sems = rest[-2:]
    depth = held.shape[0] // parts
    copies = []
    for j in range(held.shape[1] // step):
        here = slice(j * step, (j + 1) * step)
        for n in range(parts):
            rows = pl.ds(pl.multiple_of(order[n] * depth, ALIGN), depth)
            source = w_ref.at[rows, first + j * step : first + (j + 1) * step]
            target = held.at[n * depth : (n + 1) * depth, here]
            copies.append(pltpu.make_async_copy(source, target, sems.at[len(copies)]))
            copies[-1].start()
    for j in range(held.shape[1] // step):
        here = slice(j * step, (j + 1) * step)
        total = total_refs[0][:, here] if added else None
        for n in range(parts):
            copies[j * parts + n].wait()
            w = held[n * depth : (n + 1) * depth, here]
            product = jnp.dot(a_refs[n][...], w, preferred_element_type=jnp.float32)
            total = product if total is None else total + product
        for (low, high), out in zip(cuts, outs):
            out[:, here] = total[low:high].astype(out.dtype)


def project(order, parts, weight, cuts, first, width, step, added=()):
    vmem = pl.BlockSpec(memory_space=pltpu.VMEM)
    depth = parts[0].shape[1] * len(parts)
    return pl.pallas_call(
        functools.partial(project_kernel, len(parts), len(added), [c[:2] for c in cuts], first, step),
        in_specs=[pl.BlockSpec(memory_space=pltpu.SMEM)]
        + [vmem] * len(parts)
        + [pl.BlockSpec(memory_space=pltpu.HBM)]
        + [vmem] * len(added),
        out_specs=[vmem] * len(cuts),
        out_shape=[jax.ShapeDtypeStruct((high - low, width), dtype) for low, high, dtype in cuts],
        scratch_shapes=[
            pltpu.VMEM((depth, width), weight.dtype),
            pltpu.SemaphoreType.DMA((len(parts) * (width // step),)),
        ],
        compiler_params=pltpu.CompilerParams(vmem_limit_bytes=26 * 2**20),
        cost_estimate=pl.CostEstimate(
            flops=2 * parts[0].shape[0] * depth * width,
            bytes_accessed=2 * depth * width,
            transcendentals=0,
        ),
        name="project",
    )(order, *parts, in_hbm(weight), *added)


def finish_kernel(counts, *refs):
    out_ref = refs[-1]
    at = n = 0
    for count in counts:
        rows, width = refs[n].shape
        total = refs[n][...]
        for ref in refs[n + 1 : n + count]:
            total = total + ref[:rows, :].astype(jnp.float32)
        out_ref[:, at : at + width] = total.astype(out_ref.dtype)
        at += width
        n += count


def finish(chunks):
    vmem = pl.BlockSpec(memory_space=pltpu.VMEM)
    arrays = [a for chunk in chunks for a in chunk]
    width = sum(chunk[0].shape[1] for chunk in chunks)
    return pl.pallas_call(
        functools.partial(finish_kernel, [len(chunk) for chunk in chunks]),
        in_specs=[vmem] * len(arrays),
        out_specs=vmem,
        out_shape=jax.ShapeDtypeStruct((arrays[0].shape[0], width), jnp.bfloat16),
        compiler_params=pltpu.CompilerParams(vmem_limit_bytes=8 * 2**20),
        name="finish",
    )(*arrays)


def per_device(
    queries,
    cache_keys,
    cache_values,
    new_keys,
    new_values,
    out_weight,
    new_counts,
    cache_counts,
    row_dest,
):
    blocks = lax.axis_size("ctx")
    heads = lax.axis_size("head")
    me = lax.axis_index("ctx")
    my_head = lax.axis_index("head")
    block_rows = queries.shape[0]
    all_rows = block_rows * blocks
    reqs = new_counts.shape[1]
    kv_here = cache_keys.shape[1] // HEAD_DIM
    paired = blocks == 4 and kv_here % 2 == 0
    half = me % 2
    even = heads & (heads - 1) == 0
    kv = kv_here // 2 if paired else kv_here
    cols = queries.shape[1] // kv_here
    sizes = (blocks, reqs, cache_keys.shape[0], block_rows)
    caches = (cache_keys, cache_values, new_keys, new_values)

    if paired:
        near = [(i, i ^ 1) for i in range(blocks)]
        far = [(i, i ^ 2) for i in range(blocks)]
        across = [(i, i ^ 3) for i in range(blocks)]
        q_mine, q_other = split(half, queries)
        q_far = lax.ppermute(q_mine, "ctx", far)
        q_across = lax.ppermute(q_other, "ctx", across)
        packed = [
            [
                pack(half, caches, [], kv, i),
                lax.ppermute(pack(1 - half, caches, [queries], kv, i), "ctx", near),
            ]
            for i in range(kv)
        ]
        phases = [([me, me ^ 1], [q_mine]), ([me ^ 2, me ^ 3], [q_far, q_across])]
        key_blocks = [me, me ^ 1]
    else:
        rows_in = lax.all_gather(queries, "ctx", axis=0, tiled=True)
        packed = [
            [jnp.concatenate([a[:, i * HEAD_DIM : (i + 1) * HEAD_DIM] for a in caches], axis=0)]
            for i in range(kv)
        ]
        phases = [(list(range(blocks)), [rows_in])]
        key_blocks = [me]

    results = []
    for number, (query_blocks, pieces) in enumerate(phases):
        head = jnp.stack([jnp.int32(b) for b in key_blocks + query_blocks])
        numbers = jnp.concatenate([head, new_counts.reshape(-1), cache_counts.reshape(-1)])
        for i in range(kv):
            near_queries = paired and number == 0
            results.append(
                attend(
                    numbers, packed[i], pieces, cols, i, sizes, len(query_blocks), near_queries
                )
            )

    halving = heads == 4
    order = jnp.asarray([0, 2, 1, 3] if halving else list(range(heads)), jnp.int32)
    row_blocks = jnp.stack([jnp.int32(b) for p in phases for b in p[0]])
    pick = (row_blocks[:, None] == jnp.arange(blocks, dtype=jnp.int32)[None, :]).astype(jnp.int32)
    dest = jnp.sum(pick[:, :, None] * row_dest.reshape(1, blocks, block_rows), axis=1).reshape(-1)
    out_rows = all_rows // heads
    dest_head = dest // out_rows
    dest_head = dest_head ^ my_head if even else (dest_head - my_head) % heads
    place = jnp.sum((order[None, :] == dest_head[:, None]) * jnp.arange(heads)[None, :], axis=1)
    dest = (place * out_rows + dest % out_rows)[None, :].astype(jnp.int32)

    if paired:
        parts = []
        for i in range(kv):
            own, other = results[i], results[kv + i]
            from_own = [lax.ppermute(a, "ctx", far) for a in own]
            from_other = [lax.ppermute(a, "ctx", far) for a in other]
            parts.append(
                combine(
                    dest,
                    [
                        (own[0], from_other[0], own[1], from_other[1]),
                        (other[0], from_own[0], other[1], from_own[1]),
                    ],
                )
            )
        mine, others = parts, [lax.ppermute(a, "ctx", near) for a in parts]
        mine_rows = jnp.stack([half * kv + i for i in range(kv)])
        other_rows = jnp.stack([(1 - half) * kv + i for i in range(kv)])
    else:
        parts = []
        group = cols // HEAD_DIM
        landing = (jnp.arange(all_rows)[:, None] == dest).astype(jnp.bfloat16)
        for part, stat in results:
            got = lax.all_to_all(part.reshape(blocks, block_rows, cols), "ctx", 0, 0, tiled=True)
            logs = lax.all_to_all(stat.reshape(blocks, block_rows, 128), "ctx", 0, 0, tiled=True)
            logs = logs.reshape(blocks, block_rows, 128)[..., :group]
            share = jnp.exp(logs - jnp.max(logs, axis=0)[None])
            share = share / jnp.sum(share, axis=0)[None]
            stacked = got.reshape(blocks, block_rows, group, HEAD_DIM).astype(jnp.float32)
            mine = jnp.sum(share[..., None] * stacked, axis=0).astype(jnp.bfloat16)
            mine = lax.all_gather(mine.reshape(block_rows, cols), "ctx", axis=0, tiled=True)
            parts.append(jnp.dot(landing, mine, preferred_element_type=jnp.float32).astype(jnp.bfloat16))

    if not paired:
        mine, others = parts, []
        mine_rows = jnp.arange(kv, dtype=jnp.int32)

    hops = [[(i, i ^ d if even else (i + d) % heads) for i in range(heads)] for d in range(heads)]
    width = out_weight.shape[1] // 2
    step = width // 4
    direct_cuts = [
        (d * out_rows, (d + 1) * out_rows, jnp.bfloat16 if d else jnp.float32) for d in range(heads)
    ]
    pair_cuts = [
        (0, out_rows, jnp.float32),
        (out_rows, 2 * out_rows, jnp.float32),
        (2 * out_rows, 4 * out_rows, jnp.bfloat16),
    ]
    chunks = []
    for number in range(2):
        first = number * width
        by_pairs = halving and number == 0
        cuts = pair_cuts if by_pairs else direct_cuts
        if others and number == 0:
            whole = [(0, all_rows, jnp.float32)]
            begun = project(mine_rows, mine, out_weight, whole, first, width, step)
            shares = project(other_rows, others, out_weight, cuts, first, width, step, begun)
        elif others:
            rows = jnp.concatenate([mine_rows, other_rows])
            shares = project(rows, mine + others, out_weight, cuts, first, width, step)
        else:
            shares = project(mine_rows, mine, out_weight, cuts, first, width, step)
        if by_pairs:
            got = lax.ppermute(shares[2], "head", hops[1])
            away = (shares[1] + got[out_rows:].astype(jnp.float32)).astype(jnp.bfloat16)
            chunks.append([shares[0], got, lax.ppermute(away, "head", hops[2])])
        else:
            if halving:
                shares = [shares[i] for i in (0, 2, 1, 3)]
            chunks.append(
                [shares[0]] + [lax.ppermute(shares[d], "head", hops[d]) for d in range(1, heads)]
            )
    return finish(chunks)


def solution(mesh):
    return jax.shard_map(
        per_device,
        mesh=mesh,
        in_specs=(
            P(("groups", "ctx"), "head"),
            P(("groups", "ctx"), "head"),
            P(("groups", "ctx"), "head"),
            P(("groups", "ctx"), "head"),
            P(("groups", "ctx"), "head"),
            P("head", "ctx"),
            P("groups", None),
            P("groups", None),
            P("groups"),
        ),
        out_specs=P(("groups", "head"), "ctx"),
        check_vma=False,
    )
```

```python
import functools
import math

import jax
import jax.numpy as jnp
from jax import lax
from jax.experimental import pallas as pl
from jax.experimental.pallas import tpu as pltpu
from jax.sharding import PartitionSpec as P

HEAD_DIM = 128
CAPR = 512
ROWS = 16
ALIGN = 16
NEG = -1e30
SCALE = 1.0 / math.sqrt(HEAD_DIM)
LOG2E = math.log2(math.e)
SPANS = 2
COPIES = 4


def in_hbm(a):
    return pltpu.with_memory_space_constraint(a, pltpu.HBM)


def my_half():
    return lax.rem(lax.axis_index("ctx"), 2)


def pack_kernel(number, kv, other, *refs):
    sources, out_ref, sems = refs[:-2], refs[-2], refs[-1]
    block = (1 - my_half() if other else my_half()) * kv + number
    copies = []
    at = 0
    for ref in sources[:4]:
        rows = ref.shape[0]
        columns = pl.ds(pl.multiple_of(block * HEAD_DIM, HEAD_DIM), HEAD_DIM)
        copies.append((ref.at[:, columns], out_ref.at[at : at + rows, :]))
        at += rows
    for ref in sources[4:]:
        rows = ref.shape[0]
        heads = (out_ref.shape[0] - at) // rows
        for g in range(heads):
            columns = pl.ds(pl.multiple_of((block * heads + g) * HEAD_DIM, HEAD_DIM), HEAD_DIM)
            copies.append((ref.at[:, columns], out_ref.at[at : at + rows, :]))
            at += rows
    copies = [pltpu.make_async_copy(a, b, sems.at[n]) for n, (a, b) in enumerate(copies)]
    for c in copies:
        c.start()
    for c in copies:
        c.wait()


def pack(other, arrays, queries, kv, number):
    group = queries[0].shape[1] // arrays[0].shape[1] if queries else 0
    rows = sum(a.shape[0] for a in arrays) + sum(q.shape[0] * group for q in queries)
    return pl.pallas_call(
        functools.partial(pack_kernel, number, kv, other),
        in_specs=[pl.BlockSpec(memory_space=pltpu.HBM)] * (len(arrays) + len(queries)),
        out_specs=pl.BlockSpec(memory_space=pltpu.VMEM),
        out_shape=jax.ShapeDtypeStruct((rows, HEAD_DIM), arrays[0].dtype),
        scratch_shapes=[pltpu.SemaphoreType.DMA((len(arrays) + group,))],
        compiler_params=pltpu.CompilerParams(vmem_limit_bytes=4 * 2**20),
        name="pack",
    )(*[in_hbm(a) for a in (*arrays, *queries)])


def split_kernel(q_ref, *refs):
    outs, sems = refs[:-1], refs[-1]
    width = outs[0].shape[1]
    copies = []
    for n, out in enumerate(outs):
        columns = pl.ds(pl.multiple_of((my_half() ^ n) * width, width), width)
        copies.append(pltpu.make_async_copy(q_ref.at[:, columns], out, sems.at[n]))
    for c in copies:
        c.start()
    for c in copies:
        c.wait()


def split(a):
    half = jax.ShapeDtypeStruct((a.shape[0], a.shape[1] // 2), a.dtype)
    return pl.pallas_call(
        split_kernel,
        in_specs=[pl.BlockSpec(memory_space=pltpu.HBM)],
        out_specs=[pl.BlockSpec(memory_space=pltpu.VMEM)] * 2,
        out_shape=[half, half],
        scratch_shapes=[pltpu.SemaphoreType.DMA((2,))],
        compiler_params=pltpu.CompilerParams(vmem_limit_bytes=2 * 2**20),
        name="split",
    )(in_hbm(a))


def attention_kernel(
    key_blocks, query_blocks, number, window, shard_rows, block_rows, near_queries, weight_block,
    new_ref, cache_ref, weight_ref, *rest,
):
    key_blocks, row_blocks = key_blocks(), query_blocks()
    shards = len(key_blocks)
    query_blocks = len(row_blocks)
    reqs = new_ref.shape[1]
    packed = rest[:shards]
    q_refs = rest[shards : -4 - SPANS]
    out_ref, held = rest[-4 - SPANS], rest[-3 - SPANS : -3]
    sorted_q, part, sems = rest[-3:]
    copies = []
    for j, there in enumerate(held):
        rows, width = there.shape
        share = rows // COPIES
        for n in range(COPIES):
            first = pl.multiple_of(weight_block() * rows + n * share, ALIGN)
            source = weight_ref.at[pl.ds(first, share), j * width : (j + 1) * width]
            target = there.at[n * share : (n + 1) * share, :]
            copies.append(pltpu.make_async_copy(source, target, sems.at[len(copies)]))
            copies[-1].start()
    padded = sorted_q.shape[0]
    cols = sorted_q.shape[1]
    group = cols // HEAD_DIM
    all_rows = out_ref.shape[0]

    def new_counts(b, r):
        return new_ref[b, r]

    def cache_counts(b, r):
        return cache_ref[b, r]

    starts = [[jnp.int32(0)] for _ in row_blocks]
    bases = [[] for _ in row_blocks]
    tile_ends = []
    last = jnp.int32(0)
    for r in range(reqs):
        amount = jnp.int32(0)
        for b, block in enumerate(row_blocks):
            bases[b].append(amount)
            amount = amount + new_counts(block, r)
            starts[b].append(starts[b][-1] + new_counts(block, r))
        last = last + (amount + (ROWS - 1)) // ROWS
        tile_ends.append(last)
    tile_starts = [jnp.int32(0)] + tile_ends[:-1]

    offset = lax.broadcasted_iota(jnp.int32, (1, all_rows), 1)
    pos = jnp.zeros((1, all_rows), jnp.int32)
    for b in range(query_blocks):
        here = offset - b * block_rows
        for r in range(reqs):
            mine = (here >= starts[b][r]) & (here < starts[b][r + 1])
            mine = mine & (here >= 0) & (here < block_rows)
            first = tile_starts[r] * ROWS + bases[b][r] - starts[b][r]
            pos = jnp.where(mine, first + here, pos)
    sorter = (lax.broadcasted_iota(jnp.int32, (padded, all_rows), 0) == pos).astype(jnp.bfloat16)
    rows_in = [q[:, number * cols : (number + 1) * cols] for q in q_refs]
    if near_queries:
        first = 2 * (shard_rows + block_rows)
        near = [
            packed[1][first + g * block_rows : first + (g + 1) * block_rows, :]
            for g in range(group)
        ]
        rows_in.insert(1, jnp.concatenate(near, axis=1))
    rows_in = jnp.concatenate(rows_in, axis=0)
    sorted_q[...] = jnp.dot(sorter, rows_in, preferred_element_type=jnp.float32).astype(
        jnp.bfloat16
    )
    part[...] = jnp.zeros_like(part)

    width = shards * (window + block_rows)
    plain = (shards * window) // 128 * 128
    key = lax.broadcasted_iota(jnp.int32, (1, width), 1)
    lane = lax.broadcasted_iota(jnp.int32, (ROWS, 128), 1)
    ones = jnp.ones((width, HEAD_DIM), jnp.bfloat16)

    def tile(i, carry):
        r = jnp.int32(0)
        start_tile = jnp.int32(0)
        for e in tile_ends[:-1]:
            r = r + (i >= e).astype(jnp.int32)
            start_tile = jnp.where(i >= e, e, start_tile)
        inside = None
        key_pos = jnp.full((1, width), -1, jnp.int32)
        ks, vs = [], []
        for j in range(shards):
            shard = key_blocks[j]
            low = jnp.int32(0)
            new_low = jnp.int32(0)
            for o in range(reqs - 1):
                low = low + jnp.where(o < r, cache_counts(shard, o), 0)
                new_low = new_low + jnp.where(o < r, new_counts(shard, o), 0)
            high = low + cache_counts(shard, r)
            new_high = new_low + new_counts(shard, r)
            start = jnp.clip(low // ALIGN * ALIGN, 0, shard_rows - window)
            start = pl.multiple_of(start, ALIGN)
            ks.append(packed[j][pl.ds(start, window), :])
            vs.append(packed[j][pl.ds(pl.multiple_of(start + shard_rows, ALIGN), window), :])
            first = key - j * window + start
            seen = (key >= j * window) & (key < (j + 1) * window)
            seen = seen & (first >= low) & (first < high)
            inside = seen if inside is None else inside | seen
            base = shards * window + j * block_rows
            fresh = key - base
            seen = (key >= base) & (fresh < block_rows)
            key_pos = jnp.where(seen, shard * block_rows + fresh, key_pos)
            inside = inside | (seen & (fresh >= new_low) & (fresh < new_high))
        after = 2 * shard_rows
        for j in range(shards):
            ks.append(packed[j][after : after + block_rows, :])
            vs.append(packed[j][after + block_rows : after + 2 * block_rows, :])
        ks = jnp.concatenate(ks, axis=0)
        vs = jnp.concatenate(vs, axis=0)
        row0 = pl.multiple_of(i * ROWS, ROWS)
        q = jnp.concatenate(
            [
                sorted_q[pl.ds(row0, ROWS), g * HEAD_DIM : (g + 1) * HEAD_DIM]
                for g in range(group)
            ],
            axis=0,
        )
        scores = lax.dot_general(
            q, ks, (((1,), (1,)), ((), ())), preferred_element_type=jnp.float32
        )
        bias = jnp.where(inside, 0.0, NEG)
        t = jnp.zeros((ROWS, 1), jnp.int32)
        among = (i - start_tile) * ROWS + lax.broadcasted_iota(jnp.int32, (ROWS, 1), 0)
        base = jnp.int32(0)
        for block in row_blocks:
            begin = jnp.int32(0)
            for o in range(reqs - 1):
                begin = begin + jnp.where(o < r, new_counts(block, o), 0)
            t = jnp.where(among >= base, block * block_rows + begin + among - base, t)
            base = base + new_counts(block, r)
        causal = jnp.where(key_pos[:, plain:] <= t, bias[:, plain:], NEG)
        causal = jnp.concatenate([causal] * group, axis=0)
        scores = jnp.concatenate(
            [scores[:, :plain] + bias[:, :plain], scores[:, plain:] + causal], axis=1
        )
        top = jnp.max(scores, axis=1, keepdims=True)
        probs = jnp.exp2((scores - top) * (SCALE * LOG2E)).astype(jnp.bfloat16)
        mixed = jnp.dot(
            probs,
            jnp.concatenate([vs, ones], axis=1),
            preferred_element_type=jnp.float32,
        )
        total = mixed[:, HEAD_DIM:]
        value = (mixed[:, :HEAD_DIM] / total).astype(jnp.bfloat16)
        lse = top * SCALE + jnp.log(total)
        logs = jnp.zeros((ROWS, 128), jnp.float32)
        for g in range(group):
            rows = slice(g * ROWS, (g + 1) * ROWS)
            part[pl.ds(row0, ROWS), g * HEAD_DIM : (g + 1) * HEAD_DIM] = value[rows]
            logs = jnp.where(lax.rem(lane, group) == g, lse[rows], logs)
        high = logs.astype(jnp.bfloat16)
        rest_of = logs - high.astype(jnp.float32)
        middle = rest_of.astype(jnp.bfloat16)
        low = rest_of - middle.astype(jnp.float32)
        logs = jnp.where(lane < 2 * group, middle.astype(jnp.float32), low)
        logs = jnp.where(lane < group, high.astype(jnp.float32), logs)
        part[pl.ds(row0, ROWS), cols:] = logs.astype(jnp.bfloat16)
        return carry

    lax.fori_loop(0, last, tile, jnp.int32(0))

    back = (((0,), (0,)), ((), ()))
    out_ref[...] = lax.dot_general(
        sorter, part[...], back, preferred_element_type=jnp.float32
    ).astype(jnp.bfloat16)
    for c in copies:
        c.wait()


def attend(
    counts, packed, queries, cols, number, block_rows, shard_rows, key_blocks, query_blocks, near_queries,
    weight, weight_block,
):
    all_rows = len(query_blocks()) * block_rows
    reqs = counts[0].shape[1]
    padded = (all_rows + reqs * (ROWS - 1)) // ROWS * ROWS
    sets = len(packed)
    window = min(CAPR + ALIGN, shard_rows)
    vmem = pl.BlockSpec(memory_space=pltpu.VMEM)
    return pl.pallas_call(
        functools.partial(
            attention_kernel,
            key_blocks, query_blocks, number, window, shard_rows, block_rows, near_queries, weight_block,
        ),
        in_specs=[pl.BlockSpec(memory_space=pltpu.SMEM)] * 2
        + [pl.BlockSpec(memory_space=pltpu.HBM)]
        + [vmem] * (sets + len(queries)),
        out_specs=[vmem] * (1 + SPANS),
        scratch_shapes=[
            pltpu.VMEM((padded, cols), jnp.bfloat16),
            pltpu.VMEM((padded, cols + 128), jnp.bfloat16),
            pltpu.SemaphoreType.DMA((SPANS * COPIES,)),
        ],
        out_shape=[
            jax.ShapeDtypeStruct((all_rows, cols + 128), jnp.bfloat16),
            *[pltpu.VMEM((cols, weight.shape[1] // SPANS), weight.dtype)] * SPANS,
        ],
        compiler_params=pltpu.CompilerParams(vmem_limit_bytes=8 * 2**20),
        cost_estimate=pl.CostEstimate(
            flops=8 * padded * cols * sets * window,
            bytes_accessed=16 * 2**20,
            transcendentals=0,
        ),
        name="attend",
    )(*[in_hbm(c) for c in counts], in_hbm(weight), *packed, *queries)


def log_sums(pieces, group):
    pieces = pieces.astype(jnp.float32)
    return pieces[..., :group] + pieces[..., group : 2 * group] + pieces[..., 2 * group : 3 * group]


def places(dest, out_rows, heads):
    mine = lax.axis_index("head")
    head = lax.div(dest, out_rows)
    if heads & (heads - 1) == 0:
        head = head ^ mine
    else:
        head = lax.rem(head + heads - mine, heads)
    if heads == 4:
        head = jnp.where(head == 1, 2, jnp.where(head == 2, 1, head))
    return head * out_rows + lax.rem(dest, out_rows)


def combine_kernel(group, heads, dest_ref, *refs):
    sources, out_ref, gathered = refs[:-2], refs[-2], refs[-1]
    rows = out_ref.shape[0]
    cols = group * HEAD_DIM
    me = lax.axis_index("ctx")
    blocks = len(sources)
    block_rows = rows // blocks
    for n in range(0, blocks, 2):
        a_ref, b_ref = sources[n], sources[n + 1]
        sa, sb = log_sums(a_ref[:, cols:], group), log_sums(b_ref[:, cols:], group)
        best = jnp.maximum(sa, sb)
        wa, wb = jnp.exp(sa - best), jnp.exp(sb - best)
        whole = wa + wb
        wa, wb = wa / whole, wb / whole
        for g in range(group):
            at = slice(g * HEAD_DIM, (g + 1) * HEAD_DIM)
            one = wa[:, g : g + 1] * a_ref[:, at].astype(jnp.float32)
            one = one + wb[:, g : g + 1] * b_ref[:, at].astype(jnp.float32)
            one = one.astype(jnp.bfloat16)
            for k in range(2):
                first = pl.multiple_of((me ^ (n + k)) * block_rows, ALIGN)
                gathered[pl.ds(first, block_rows), at] = one[k * block_rows : (k + 1) * block_rows]
    dest = places(dest_ref[...].reshape(1, rows), rows // heads, heads)
    landing = (lax.broadcasted_iota(jnp.int32, (rows, rows), 0) == dest).astype(jnp.bfloat16)
    out_ref[...] = jnp.dot(landing, gathered[...], preferred_element_type=jnp.float32).astype(
        jnp.bfloat16
    )


def combine(dest, arrays, heads):
    vmem = pl.BlockSpec(memory_space=pltpu.VMEM)
    cols = arrays[0].shape[1] - 128
    return pl.pallas_call(
        functools.partial(combine_kernel, cols // HEAD_DIM, heads),
        in_specs=[vmem] * (1 + len(arrays)),
        out_specs=vmem,
        out_shape=jax.ShapeDtypeStruct((dest.shape[0], cols), jnp.bfloat16),
        scratch_shapes=[pltpu.VMEM((dest.shape[0], cols), jnp.bfloat16)],
        compiler_params=pltpu.CompilerParams(vmem_limit_bytes=6 * 2**20),
        name="combine",
    )(dest, *arrays)


def project_kernel(parts, added, cuts, step, *refs):
    a_refs, w_refs = refs[:parts], refs[parts : 2 * parts]
    total_refs, outs = refs[2 * parts : 2 * parts + added], refs[2 * parts + added :]

    def columns(j, carry):
        here = pl.ds(pl.multiple_of(j * step, step), step)
        total = total_refs[0][:, here] if added else None
        for a, w in zip(a_refs, w_refs):
            product = jnp.dot(a[...], w[:, here], preferred_element_type=jnp.float32)
            total = product if total is None else total + product
        for (low, high), out in zip(cuts, outs):
            out[:, here] = total[low:high].astype(out.dtype)
        return carry

    lax.fori_loop(0, outs[0].shape[1] // step, columns, 0)


def project(parts, weights, cuts, step, added=()):
    vmem = pl.BlockSpec(memory_space=pltpu.VMEM)
    depth = parts[0].shape[1] * len(parts)
    width = weights[0].shape[1]
    return pl.pallas_call(
        functools.partial(project_kernel, len(parts), len(added), [c[:2] for c in cuts], step),
        in_specs=[vmem] * (2 * len(parts) + len(added)),
        out_specs=[vmem] * len(cuts),
        out_shape=[jax.ShapeDtypeStruct((high - low, width), dtype) for low, high, dtype in cuts],
        compiler_params=pltpu.CompilerParams(vmem_limit_bytes=6 * 2**20),
        cost_estimate=pl.CostEstimate(
            flops=4 * parts[0].shape[0] * depth * width,
            bytes_accessed=depth * width,
            transcendentals=0,
        ),
        name="project",
    )(*parts, *[pltpu.with_memory_space_constraint(w, pltpu.VMEM) for w in weights], *added)


def finish_kernel(counts, *refs):
    out_ref = refs[-1]
    at = n = 0
    for count in counts:
        rows, width = refs[n].shape
        total = refs[n][...]
        for ref in refs[n + 1 : n + count]:
            total = total + ref[:rows, :].astype(jnp.float32)
        out_ref[:, at : at + width] = total.astype(out_ref.dtype)
        at += width
        n += count


def finish(chunks):
    vmem = pl.BlockSpec(memory_space=pltpu.VMEM)
    arrays = [a for chunk in chunks for a in chunk]
    width = sum(chunk[0].shape[1] for chunk in chunks)
    return pl.pallas_call(
        functools.partial(finish_kernel, [len(chunk) for chunk in chunks]),
        in_specs=[vmem] * len(arrays),
        out_specs=vmem,
        out_shape=jax.ShapeDtypeStruct((arrays[0].shape[0], width), jnp.bfloat16),
        compiler_params=pltpu.CompilerParams(vmem_limit_bytes=8 * 2**20),
        name="finish",
    )(*arrays)


def per_device(
    queries,
    cache_keys,
    cache_values,
    new_keys,
    new_values,
    out_weight,
    new_counts,
    cache_counts,
    row_dest,
):
    blocks = lax.axis_size("ctx")
    heads = lax.axis_size("head")
    block_rows = queries.shape[0]
    all_rows = block_rows * blocks
    kv_here = cache_keys.shape[1] // HEAD_DIM
    paired = blocks == 4 and kv_here % 2 == 0
    even = heads & (heads - 1) == 0
    kv = kv_here // 2 if paired else kv_here
    cols = queries.shape[1] // kv_here
    shard_rows = cache_keys.shape[0]
    caches = (cache_keys, cache_values, new_keys, new_values)

    if paired:
        near = [(i, i ^ 1) for i in range(blocks)]
        far = [(i, i ^ 2) for i in range(blocks)]
        across = [(i, i ^ 3) for i in range(blocks)]
        q_mine, q_other = split(queries)
        q_far = lax.ppermute(q_mine, "ctx", far)
        q_across = lax.ppermute(q_other, "ctx", across)
        packed = [
            [
                pack(False, caches, [], kv, i),
                lax.ppermute(pack(True, caches, [queries], kv, i), "ctx", near),
            ]
            for i in range(kv)
        ]
        nearby = lambda ds: lambda: [lax.axis_index("ctx") ^ d for d in ds]
        phases = [
            (nearby((0, 1)), [q_mine], lambda i: lambda: my_half() * kv + i),
            (nearby((2, 3)), [q_far, q_across], lambda i: lambda: (1 - my_half()) * kv + i),
        ]
        key_blocks = nearby((0, 1))
    else:
        rows_in = lax.all_gather(queries, "ctx", axis=0, tiled=True)
        packed = [
            [jnp.concatenate([a[:, i * HEAD_DIM : (i + 1) * HEAD_DIM] for a in caches], axis=0)]
            for i in range(kv)
        ]
        phases = [(lambda: list(range(blocks)), [rows_in], lambda i: lambda: i)]
        key_blocks = lambda: [lax.axis_index("ctx")]

    counts = (new_counts, cache_counts)
    results = [
        attend(
            counts, packed[i], pieces, cols, i, block_rows, shard_rows, key_blocks, query_blocks,
            paired and number == 0, out_weight, weight_block(i),
        )
        for number, (query_blocks, pieces, weight_block) in enumerate(phases)
        for i in range(kv)
    ]
    weights = [r[1:] for r in results]
    results = [r[0] for r in results]
    halving = heads == 4
    out_rows = all_rows // heads

    if paired:
        mine = []
        for i in range(kv):
            own, other = results[i], results[kv + i]
            from_own, from_other = lax.ppermute(own, "ctx", far), lax.ppermute(other, "ctx", far)
            mine.append(combine(row_dest, [own, from_other, other, from_own], heads))
        others = [lax.ppermute(a, "ctx", near) for a in mine]
    else:
        mine, others = [], []
        group = cols // HEAD_DIM
        landing = jnp.arange(all_rows)[:, None] == places(row_dest, out_rows, heads)[None, :]
        for part in results:
            got = lax.all_to_all(
                part.reshape(blocks, block_rows, cols + 128), "ctx", 0, 0, tiled=True
            ).reshape(blocks, block_rows, cols + 128)
            logs = log_sums(got[..., cols:], group)
            share = jnp.exp(logs - jnp.max(logs, axis=0)[None])
            share = share / jnp.sum(share, axis=0)[None]
            stacked = got[..., :cols].reshape(blocks, block_rows, group, HEAD_DIM)
            one = jnp.sum(share[..., None] * stacked.astype(jnp.float32), axis=0)
            one = one.astype(jnp.bfloat16).reshape(block_rows, cols)
            one = lax.all_gather(one, "ctx", axis=0, tiled=True)
            mine.append(
                jnp.dot(landing.astype(one.dtype), one, preferred_element_type=jnp.float32).astype(
                    one.dtype
                )
            )

    hops = [[(i, i ^ d if even else (i + d) % heads) for i in range(heads)] for d in range(heads)]
    step = out_weight.shape[1] // SPANS // 4
    direct_cuts = [
        (d * out_rows, (d + 1) * out_rows, jnp.bfloat16 if d else jnp.float32) for d in range(heads)
    ]
    pair_cuts = [
        (0, out_rows, jnp.float32),
        (out_rows, 2 * out_rows, jnp.float32),
        (2 * out_rows, 4 * out_rows, jnp.bfloat16),
    ]
    chunks = []
    for number in range(SPANS):
        span = [w[number] for w in weights]
        by_pairs = halving and number == 0
        cuts = pair_cuts if by_pairs else direct_cuts
        if others and number == 0:
            whole = [(0, all_rows, jnp.float32)]
            begun = project(mine, span[:kv], whole, step)
            shares = project(others, span[kv:], cuts, step, begun)
        elif others:
            shares = project(mine + others, span, cuts, step)
        else:
            shares = project(mine, span, cuts, step)
        if by_pairs:
            got = lax.ppermute(shares[2], "head", hops[1])
            away = (shares[1] + got[out_rows:].astype(jnp.float32)).astype(jnp.bfloat16)
            chunks.append([shares[0], got, lax.ppermute(away, "head", hops[2])])
        else:
            if halving:
                shares = [shares[i] for i in (0, 2, 1, 3)]
            chunks.append(
                [shares[0]] + [lax.ppermute(shares[d], "head", hops[d]) for d in range(1, heads)]
            )
    return finish(chunks)


def solution(mesh):
    return jax.shard_map(
        per_device,
        mesh=mesh,
        in_specs=(
            P(("groups", "ctx"), "head"),
            P(("groups", "ctx"), "head"),
            P(("groups", "ctx"), "head"),
            P(("groups", "ctx"), "head"),
            P(("groups", "ctx"), "head"),
            P("head", "ctx"),
            P("groups", None),
            P("groups", None),
            P("groups"),
        ),
        out_specs=P(("groups", "head"), "ctx"),
        check_vma=False,
    )
```

```python
import functools
import math

import jax
import jax.numpy as jnp
from jax import lax
from jax.experimental import pallas as pl
from jax.experimental.pallas import tpu as pltpu
from jax.sharding import PartitionSpec as P

HEAD_DIM = 128
CAPR = 512
ROWS = 16
ALIGN = 16
CHAINS = 2
NEG = -1e30
SCALE = 1.0 / math.sqrt(HEAD_DIM)
LOG2E = math.log2(math.e)
SPANS = 2
COPIES = 4


def moves(*arrays):
    return pl.CostEstimate(
        flops=0, bytes_accessed=sum(2 * a.size * a.dtype.itemsize for a in arrays), transcendentals=0
    )


def in_hbm(a):
    return pltpu.with_memory_space_constraint(a, pltpu.HBM)


def my_half():
    return lax.rem(lax.axis_index("ctx"), 2)


def pack_kernel(number, kv, other, *refs):
    sources, out_ref, sems = refs[:-2], refs[-2], refs[-1]
    block = (1 - my_half() if other else my_half()) * kv + number
    copies = []
    at = 0
    for ref in sources[:4]:
        rows = ref.shape[0]
        columns = pl.ds(pl.multiple_of(block * HEAD_DIM, HEAD_DIM), HEAD_DIM)
        copies.append((ref.at[:, columns], out_ref.at[at : at + rows, :]))
        at += rows
    for ref in sources[4:]:
        rows = ref.shape[0]
        heads = (out_ref.shape[0] - at) // rows
        for g in range(heads):
            first = (number * heads + g) * HEAD_DIM
            copies.append((ref.at[:, first : first + HEAD_DIM], out_ref.at[at : at + rows, :]))
            at += rows
    copies = [pltpu.make_async_copy(a, b, sems.at[n]) for n, (a, b) in enumerate(copies)]
    for c in copies:
        c.start()
    for c in copies:
        c.wait()


def pack(other, arrays, queries, kv, number):
    group = queries[0].shape[1] // HEAD_DIM // kv if queries else 0
    rows = sum(a.shape[0] for a in arrays) + sum(q.shape[0] * group for q in queries)
    return pl.pallas_call(
        functools.partial(pack_kernel, number, kv, other),
        in_specs=[pl.BlockSpec(memory_space=pltpu.HBM)] * len(arrays)
        + [pl.BlockSpec(memory_space=pltpu.VMEM)] * len(queries),
        out_specs=pl.BlockSpec(memory_space=pltpu.VMEM),
        out_shape=jax.ShapeDtypeStruct((rows, HEAD_DIM), arrays[0].dtype),
        scratch_shapes=[pltpu.SemaphoreType.DMA((len(arrays) + group,))],
        compiler_params=pltpu.CompilerParams(vmem_limit_bytes=4 * 2**20),
        cost_estimate=moves(jax.ShapeDtypeStruct((rows, HEAD_DIM), arrays[0].dtype)),
        name="pack",
    )(*[in_hbm(a) for a in arrays], *queries)


def split_kernel(q_ref, *refs):
    outs, sems = refs[:-1], refs[-1]
    width = outs[0].shape[1]
    copies = []
    for n, out in enumerate(outs):
        columns = pl.ds(pl.multiple_of((my_half() ^ n) * width, width), width)
        copies.append(pltpu.make_async_copy(q_ref.at[:, columns], out, sems.at[n]))
    for c in copies:
        c.start()
    for c in copies:
        c.wait()


def split(a):
    half = jax.ShapeDtypeStruct((a.shape[0], a.shape[1] // 2), a.dtype)
    return pl.pallas_call(
        split_kernel,
        in_specs=[pl.BlockSpec(memory_space=pltpu.HBM)],
        out_specs=[pl.BlockSpec(memory_space=pltpu.VMEM)] * 2,
        out_shape=[half, half],
        scratch_shapes=[pltpu.SemaphoreType.DMA((2,))],
        compiler_params=pltpu.CompilerParams(vmem_limit_bytes=2 * 2**20),
        cost_estimate=moves(a),
        name="split",
    )(in_hbm(a))


def attention_kernel(
    key_blocks, query_blocks, number, window, shard_rows, block_rows, near_queries, weight_block,
    new_ref, cache_ref, weight_ref, *rest,
):
    key_blocks, row_blocks = key_blocks(), query_blocks()
    shards = len(key_blocks)
    query_blocks = len(row_blocks)
    reqs = new_ref.shape[1]
    packed = rest[:shards]
    q_refs = rest[shards : -4 - SPANS]
    out_ref, held = rest[-4 - SPANS], rest[-3 - SPANS : -3]
    sorted_q, part, sems = rest[-3:]
    copies = []
    for j, there in enumerate(held):
        rows, width = there.shape
        share = rows // COPIES
        for n in range(COPIES):
            first = pl.multiple_of(weight_block() * rows + n * share, ALIGN)
            source = weight_ref.at[pl.ds(first, share), j * width : (j + 1) * width]
            target = there.at[n * share : (n + 1) * share, :]
            copies.append(pltpu.make_async_copy(source, target, sems.at[len(copies)]))
            copies[-1].start()
    padded = sorted_q.shape[0]
    cols = sorted_q.shape[1]
    group = cols // HEAD_DIM
    all_rows = out_ref.shape[0]

    def new_counts(b, r):
        return new_ref[b, r]

    def cache_counts(b, r):
        return cache_ref[b, r]

    starts = [[jnp.int32(0)] for _ in row_blocks]
    bases = [[] for _ in row_blocks]
    tile_ends = []
    last = jnp.int32(0)
    for r in range(reqs):
        amount = jnp.int32(0)
        for b, block in enumerate(row_blocks):
            bases[b].append(amount)
            amount = amount + new_counts(block, r)
            starts[b].append(starts[b][-1] + new_counts(block, r))
        last = last + (amount + (ROWS - 1)) // ROWS
        tile_ends.append(last)
    tile_starts = [jnp.int32(0)] + tile_ends[:-1]

    offset = lax.broadcasted_iota(jnp.int32, (1, all_rows), 1)
    pos = jnp.zeros((1, all_rows), jnp.int32)
    for b in range(query_blocks):
        here = offset - b * block_rows
        for r in range(reqs):
            mine = (here >= starts[b][r]) & (here < starts[b][r + 1])
            mine = mine & (here >= 0) & (here < block_rows)
            first = tile_starts[r] * ROWS + bases[b][r] - starts[b][r]
            pos = jnp.where(mine, first + here, pos)
    sorter = (lax.broadcasted_iota(jnp.int32, (padded, all_rows), 0) == pos).astype(jnp.bfloat16)
    rows_in = [q[:, number * cols : (number + 1) * cols] for q in q_refs]
    if near_queries:
        first = 2 * (shard_rows + block_rows)
        near = [
            packed[1][first + g * block_rows : first + (g + 1) * block_rows, :]
            for g in range(group)
        ]
        rows_in.insert(1, jnp.concatenate(near, axis=1))
    rows_in = jnp.concatenate(rows_in, axis=0)
    sorted_q[...] = jnp.dot(sorter, rows_in, preferred_element_type=jnp.float32).astype(
        jnp.bfloat16
    )
    part[...] = jnp.zeros_like(part)

    width = shards * (window + block_rows)
    plain = (shards * window) // 128 * 128
    key = lax.broadcasted_iota(jnp.int32, (1, width), 1)
    lane = lax.broadcasted_iota(jnp.int32, (ROWS, 128), 1)
    ones = jnp.ones((width, HEAD_DIM), jnp.bfloat16)

    def tile(i, carry):
        r = jnp.int32(0)
        start_tile = jnp.int32(0)
        for e in tile_ends[:-1]:
            r = r + (i >= e).astype(jnp.int32)
            start_tile = jnp.where(i >= e, e, start_tile)
        inside = None
        key_pos = jnp.full((1, width), -1, jnp.int32)
        ks, vs = [], []
        for j in range(shards):
            shard = key_blocks[j]
            low = jnp.int32(0)
            new_low = jnp.int32(0)
            for o in range(reqs - 1):
                low = low + jnp.where(o < r, cache_counts(shard, o), 0)
                new_low = new_low + jnp.where(o < r, new_counts(shard, o), 0)
            high = low + cache_counts(shard, r)
            new_high = new_low + new_counts(shard, r)
            start = jnp.clip(low // ALIGN * ALIGN, 0, shard_rows - window)
            start = pl.multiple_of(start, ALIGN)
            ks.append(packed[j][pl.ds(start, window), :])
            vs.append(packed[j][pl.ds(pl.multiple_of(start + shard_rows, ALIGN), window), :])
            first = key - j * window + start
            seen = (key >= j * window) & (key < (j + 1) * window)
            seen = seen & (first >= low) & (first < high)
            inside = seen if inside is None else inside | seen
            base = shards * window + j * block_rows
            fresh = key - base
            seen = (key >= base) & (fresh < block_rows)
            key_pos = jnp.where(seen, shard * block_rows + fresh, key_pos)
            inside = inside | (seen & (fresh >= new_low) & (fresh < new_high))
        after = 2 * shard_rows
        for j in range(shards):
            ks.append(packed[j][after : after + block_rows, :])
            vs.append(packed[j][after + block_rows : after + 2 * block_rows, :])
        ks = jnp.concatenate(ks, axis=0)
        vs = jnp.concatenate(vs, axis=0)
        row0 = pl.multiple_of(i * ROWS, ROWS)
        bias = jnp.where(inside, 0.0, NEG)
        t = jnp.zeros((ROWS, 1), jnp.int32)
        among = (i - start_tile) * ROWS + lax.broadcasted_iota(jnp.int32, (ROWS, 1), 0)
        base = jnp.int32(0)
        for block in row_blocks:
            begin = jnp.int32(0)
            for o in range(reqs - 1):
                begin = begin + jnp.where(o < r, new_counts(block, o), 0)
            t = jnp.where(among >= base, block * block_rows + begin + among - base, t)
            base = base + new_counts(block, r)
        causal = jnp.where(key_pos[:, plain:] <= t, bias[:, plain:], NEG)
        values = jnp.concatenate([vs, ones], axis=1)
        logs = jnp.zeros((ROWS, 128), jnp.float32)
        together = group // CHAINS if group % CHAINS == 0 else group
        causal = jnp.concatenate([causal] * together, axis=0)
        for chain in range(0, group, together):
            heads = range(chain, chain + together)
            q = jnp.concatenate(
                [sorted_q[pl.ds(row0, ROWS), g * HEAD_DIM : (g + 1) * HEAD_DIM] for g in heads], axis=0
            )
            scores = lax.dot_general(
                q, ks, (((1,), (1,)), ((), ())), preferred_element_type=jnp.float32
            )
            scores = jnp.concatenate(
                [scores[:, :plain] + bias[:, :plain], scores[:, plain:] + causal], axis=1
            )
            top = jnp.max(scores, axis=1, keepdims=True)
            probs = jnp.exp2((scores - top) * (SCALE * LOG2E)).astype(jnp.bfloat16)
            mixed = jnp.dot(probs, values, preferred_element_type=jnp.float32)
            total = mixed[:, HEAD_DIM:]
            value = (mixed[:, :HEAD_DIM] / total).astype(jnp.bfloat16)
            lse = top * SCALE + jnp.log(total)
            for n, g in enumerate(heads):
                rows = slice(n * ROWS, (n + 1) * ROWS)
                part[pl.ds(row0, ROWS), g * HEAD_DIM : (g + 1) * HEAD_DIM] = value[rows]
                logs = jnp.where(lax.rem(lane, group) == g, lse[rows], logs)
        high = logs.astype(jnp.bfloat16)
        rest_of = logs - high.astype(jnp.float32)
        middle = rest_of.astype(jnp.bfloat16)
        low = rest_of - middle.astype(jnp.float32)
        logs = jnp.where(lane < 2 * group, middle.astype(jnp.float32), low)
        logs = jnp.where(lane < group, high.astype(jnp.float32), logs)
        part[pl.ds(row0, ROWS), cols:] = logs.astype(jnp.bfloat16)
        return carry

    lax.fori_loop(0, last, tile, jnp.int32(0))

    back = (((0,), (0,)), ((), ()))
    out_ref[...] = lax.dot_general(
        sorter, part[...], back, preferred_element_type=jnp.float32
    ).astype(jnp.bfloat16)
    for c in copies:
        c.wait()


def attend(
    counts, packed, queries, cols, number, block_rows, shard_rows, key_blocks, query_blocks, near_queries,
    weight, weight_block,
):
    all_rows = len(query_blocks()) * block_rows
    reqs = counts[0].shape[1]
    padded = (all_rows + reqs * (ROWS - 1)) // ROWS * ROWS
    sets = len(packed)
    window = min(CAPR + ALIGN, shard_rows)
    vmem = pl.BlockSpec(memory_space=pltpu.VMEM)
    return pl.pallas_call(
        functools.partial(
            attention_kernel,
            key_blocks, query_blocks, number, window, shard_rows, block_rows, near_queries, weight_block,
        ),
        in_specs=[pl.BlockSpec(memory_space=pltpu.SMEM)] * 2
        + [pl.BlockSpec(memory_space=pltpu.HBM)]
        + [vmem] * (sets + len(queries)),
        out_specs=[vmem] * (1 + SPANS),
        scratch_shapes=[
            pltpu.VMEM((padded, cols), jnp.bfloat16),
            pltpu.VMEM((padded, cols + 128), jnp.bfloat16),
            pltpu.SemaphoreType.DMA((SPANS * COPIES,)),
        ],
        out_shape=[
            jax.ShapeDtypeStruct((all_rows, cols + 128), jnp.bfloat16),
            *[pltpu.VMEM((cols, weight.shape[1] // SPANS), weight.dtype)] * SPANS,
        ],
        compiler_params=pltpu.CompilerParams(vmem_limit_bytes=8 * 2**20),
        cost_estimate=pl.CostEstimate(
            flops=8 * padded * cols * sets * window,
            bytes_accessed=16 * 2**20,
            transcendentals=0,
        ),
        name="attend",
    )(*[in_hbm(c) for c in counts], in_hbm(weight), *packed, *queries)


def log_sums(pieces, group):
    pieces = pieces.astype(jnp.float32)
    return pieces[..., :group] + pieces[..., group : 2 * group] + pieces[..., 2 * group : 3 * group]


def places(dest, out_rows, heads):
    mine = lax.axis_index("head")
    head = lax.div(dest, out_rows)
    if heads & (heads - 1) == 0:
        head = head ^ mine
    else:
        head = lax.rem(head + heads - mine, heads)
    if heads == 4:
        head = jnp.where(head == 1, 2, jnp.where(head == 2, 1, head))
    return head * out_rows + lax.rem(dest, out_rows)


def mixed_head(a_ref, b_ref, g, weights):
    at = slice(g * HEAD_DIM, (g + 1) * HEAD_DIM)
    one = weights[0][:, g : g + 1] * a_ref[:, at].astype(jnp.float32)
    one = one + weights[1][:, g : g + 1] * b_ref[:, at].astype(jnp.float32)
    return one.astype(jnp.bfloat16)


def mixing_weights(a_ref, b_ref, group):
    cols = group * HEAD_DIM
    sa, sb = log_sums(a_ref[:, cols:], group), log_sums(b_ref[:, cols:], group)
    best = jnp.maximum(sa, sb)
    wa, wb = jnp.exp(sa - best), jnp.exp(sb - best)
    whole = wa + wb
    return wa / whole, wb / whole


def mix_kernel(group, a_ref, b_ref, out_ref):
    weights = mixing_weights(a_ref, b_ref, group)
    for g in range(group):
        out_ref[:, g * HEAD_DIM : (g + 1) * HEAD_DIM] = mixed_head(a_ref, b_ref, g, weights)


def mix(a, b):
    vmem = pl.BlockSpec(memory_space=pltpu.VMEM)
    cols = a.shape[1] - 128
    return pl.pallas_call(
        functools.partial(mix_kernel, cols // HEAD_DIM),
        in_specs=[vmem] * 2,
        out_specs=vmem,
        out_shape=jax.ShapeDtypeStruct((a.shape[0], cols), jnp.bfloat16),
        compiler_params=pltpu.CompilerParams(vmem_limit_bytes=4 * 2**20),
        cost_estimate=moves(a, b),
        name="mix",
    )(a, b)


def combine_kernel(group, heads, dest_ref, a_ref, b_ref, far_ref, out_ref, gathered):
    rows = out_ref.shape[0]
    half_rows = a_ref.shape[0]
    block_rows = half_rows // 2
    me = lax.axis_index("ctx")
    weights = mixing_weights(a_ref, b_ref, group)
    dest = places(dest_ref[...].reshape(1, rows), rows // heads, heads)
    landing = (lax.broadcasted_iota(jnp.int32, (rows, rows), 0) == dest).astype(jnp.bfloat16)
    first = [pl.multiple_of((me ^ n) * block_rows, ALIGN) for n in range(4)]
    for g in range(group):
        at = slice(g * HEAD_DIM, (g + 1) * HEAD_DIM)
        one = mixed_head(a_ref, b_ref, g, weights)
        for k in range(2):
            here = slice(k * block_rows, (k + 1) * block_rows)
            gathered[pl.ds(first[k], block_rows), at] = one[here]
            gathered[pl.ds(first[2 + k], block_rows), at] = far_ref[here, at]
    out_ref[...] = jnp.dot(landing, gathered[...], preferred_element_type=jnp.float32).astype(
        jnp.bfloat16
    )


def combine(dest, a, b, far, heads):
    vmem = pl.BlockSpec(memory_space=pltpu.VMEM)
    cols = far.shape[1]
    return pl.pallas_call(
        functools.partial(combine_kernel, cols // HEAD_DIM, heads),
        in_specs=[vmem] * 4,
        out_specs=vmem,
        out_shape=jax.ShapeDtypeStruct((dest.shape[0], cols), jnp.bfloat16),
        scratch_shapes=[pltpu.VMEM((dest.shape[0], cols), jnp.bfloat16)],
        compiler_params=pltpu.CompilerParams(vmem_limit_bytes=6 * 2**20),
        cost_estimate=moves(a, b, far),
        name="combine",
    )(dest, a, b, far)


def project_kernel(parts, added, cuts, step, *refs):
    a_refs, w_refs = refs[:parts], refs[parts : 2 * parts]
    total_refs, outs = refs[2 * parts : 2 * parts + added], refs[2 * parts + added :]

    def columns(j, carry):
        here = pl.ds(pl.multiple_of(j * step, step), step)
        total = total_refs[0][:, here] if added else None
        for a, w in zip(a_refs, w_refs):
            product = jnp.dot(a[...], w[:, here], preferred_element_type=jnp.float32)
            total = product if total is None else total + product
        for (low, high), out in zip(cuts, outs):
            out[:, here] = total[low:high].astype(out.dtype)
        return carry

    lax.fori_loop(0, outs[0].shape[1] // step, columns, 0)


def project(parts, weights, cuts, step, added=()):
    vmem = pl.BlockSpec(memory_space=pltpu.VMEM)
    depth = parts[0].shape[1] * len(parts)
    width = weights[0].shape[1]
    return pl.pallas_call(
        functools.partial(project_kernel, len(parts), len(added), [c[:2] for c in cuts], step),
        in_specs=[vmem] * (2 * len(parts) + len(added)),
        out_specs=[vmem] * len(cuts),
        out_shape=[jax.ShapeDtypeStruct((high - low, width), dtype) for low, high, dtype in cuts],
        compiler_params=pltpu.CompilerParams(vmem_limit_bytes=6 * 2**20),
        cost_estimate=pl.CostEstimate(
            flops=4 * parts[0].shape[0] * depth * width,
            bytes_accessed=depth * width,
            transcendentals=0,
        ),
        name="project",
    )(*parts, *[pltpu.with_memory_space_constraint(w, pltpu.VMEM) for w in weights], *added)


def finish_kernel(counts, *refs):
    out_ref = refs[-1]
    at = n = 0
    for count in counts:
        rows, width = refs[n].shape
        total = refs[n][...]
        for ref in refs[n + 1 : n + count]:
            total = total + ref[:rows, :].astype(jnp.float32)
        out_ref[:, at : at + width] = total.astype(out_ref.dtype)
        at += width
        n += count


def finish(chunks):
    vmem = pl.BlockSpec(memory_space=pltpu.VMEM)
    arrays = [a for chunk in chunks for a in chunk]
    width = sum(chunk[0].shape[1] for chunk in chunks)
    return pl.pallas_call(
        functools.partial(finish_kernel, [len(chunk) for chunk in chunks]),
        in_specs=[vmem] * len(arrays),
        out_specs=vmem,
        out_shape=jax.ShapeDtypeStruct((arrays[0].shape[0], width), jnp.bfloat16),
        compiler_params=pltpu.CompilerParams(vmem_limit_bytes=8 * 2**20),
        name="finish",
    )(*arrays)


def per_device(
    queries,
    cache_keys,
    cache_values,
    new_keys,
    new_values,
    out_weight,
    new_counts,
    cache_counts,
    row_dest,
):
    blocks = lax.axis_size("ctx")
    heads = lax.axis_size("head")
    block_rows = queries.shape[0]
    all_rows = block_rows * blocks
    kv_here = cache_keys.shape[1] // HEAD_DIM
    paired = blocks == 4 and kv_here % 2 == 0
    even = heads & (heads - 1) == 0
    kv = kv_here // 2 if paired else kv_here
    cols = queries.shape[1] // kv_here
    shard_rows = cache_keys.shape[0]
    caches = (cache_keys, cache_values, new_keys, new_values)

    if paired:
        near = [(i, i ^ 1) for i in range(blocks)]
        far = [(i, i ^ 2) for i in range(blocks)]
        across = [(i, i ^ 3) for i in range(blocks)]
        q_mine, q_other = split(queries)
        q_far = lax.ppermute(q_mine, "ctx", far)
        q_across = lax.ppermute(q_other, "ctx", across)
        packed = [
            [
                pack(False, caches, [], kv, i),
                lax.ppermute(pack(True, caches, [q_other], kv, i), "ctx", near),
            ]
            for i in range(kv)
        ]
        nearby = lambda ds: lambda: [lax.axis_index("ctx") ^ d for d in ds]
        phases = [
            (nearby((0, 1)), [q_mine], lambda i: lambda: my_half() * kv + i),
            (nearby((2, 3)), [q_far, q_across], lambda i: lambda: (1 - my_half()) * kv + i),
        ]
        key_blocks = nearby((0, 1))
    else:
        rows_in = lax.all_gather(queries, "ctx", axis=0, tiled=True)
        packed = [
            [jnp.concatenate([a[:, i * HEAD_DIM : (i + 1) * HEAD_DIM] for a in caches], axis=0)]
            for i in range(kv)
        ]
        phases = [(lambda: list(range(blocks)), [rows_in], lambda i: lambda: i)]
        key_blocks = lambda: [lax.axis_index("ctx")]

    counts = (new_counts, cache_counts)
    results = [
        attend(
            counts, packed[i], pieces, cols, i, block_rows, shard_rows, key_blocks, query_blocks,
            paired and number == 0, out_weight, weight_block(i),
        )
        for number, (query_blocks, pieces, weight_block) in enumerate(phases)
        for i in range(kv)
    ]
    weights = [r[1:] for r in results]
    results = [r[0] for r in results]
    halving = heads == 4
    out_rows = all_rows // heads

    if paired:
        mine = []
        for i in range(kv):
            own, other = results[i], results[kv + i]
            from_own, from_other = lax.ppermute(own, "ctx", far), lax.ppermute(other, "ctx", far)
            mine.append(combine(row_dest, own, from_other, mix(other, from_own), heads))
        others = [lax.ppermute(a, "ctx", near) for a in mine]
    else:
        mine, others = [], []
        group = cols // HEAD_DIM
        landing = jnp.arange(all_rows)[:, None] == places(row_dest, out_rows, heads)[None, :]
        for part in results:
            got = lax.all_to_all(
                part.reshape(blocks, block_rows, cols + 128), "ctx", 0, 0, tiled=True
            ).reshape(blocks, block_rows, cols + 128)
            logs = log_sums(got[..., cols:], group)
            share = jnp.exp(logs - jnp.max(logs, axis=0)[None])
            share = share / jnp.sum(share, axis=0)[None]
            stacked = got[..., :cols].reshape(blocks, block_rows, group, HEAD_DIM)
            one = jnp.sum(share[..., None] * stacked.astype(jnp.float32), axis=0)
            one = one.astype(jnp.bfloat16).reshape(block_rows, cols)
            one = lax.all_gather(one, "ctx", axis=0, tiled=True)
            mine.append(
                jnp.dot(landing.astype(one.dtype), one, preferred_element_type=jnp.float32).astype(
                    one.dtype
                )
            )

    hops = [[(i, i ^ d if even else (i + d) % heads) for i in range(heads)] for d in range(heads)]
    step = out_weight.shape[1] // SPANS // 4
    direct_cuts = [
        (d * out_rows, (d + 1) * out_rows, jnp.bfloat16 if d else jnp.float32) for d in range(heads)
    ]
    pair_cuts = [
        (0, out_rows, jnp.float32),
        (out_rows, 2 * out_rows, jnp.float32),
        (2 * out_rows, 4 * out_rows, jnp.bfloat16),
    ]
    chunks = []
    for number in range(SPANS):
        span = [w[number] for w in weights]
        by_pairs = halving and number == 0
        cuts = pair_cuts if by_pairs else direct_cuts
        if others and number == 0:
            whole = [(0, all_rows, jnp.float32)]
            begun = project(mine, span[:kv], whole, step)
            shares = project(others, span[kv:], cuts, step, begun)
        elif others:
            shares = project(mine + others, span, cuts, step)
        else:
            shares = project(mine, span, cuts, step)
        if by_pairs:
            got = lax.ppermute(shares[2], "head", hops[1])
            away = (shares[1] + got[out_rows:].astype(jnp.float32)).astype(jnp.bfloat16)
            chunks.append([shares[0], got, lax.ppermute(away, "head", hops[2])])
        else:
            if halving:
                shares = [shares[i] for i in (0, 2, 1, 3)]
            chunks.append(
                [shares[0]] + [lax.ppermute(shares[d], "head", hops[d]) for d in range(1, heads)]
            )
    return finish(chunks)


def solution(mesh):
    return jax.shard_map(
        per_device,
        mesh=mesh,
        in_specs=(
            P(("groups", "ctx"), "head"),
            P(("groups", "ctx"), "head"),
            P(("groups", "ctx"), "head"),
            P(("groups", "ctx"), "head"),
            P(("groups", "ctx"), "head"),
            P("head", "ctx"),
            P("groups", None),
            P("groups", None),
            P("groups"),
        ),
        out_specs=P(("groups", "head"), "ctx"),
        check_vma=False,
    )
```

```python
import functools
import math

import jax
import jax.numpy as jnp
from jax import lax
from jax.experimental import pallas as pl
from jax.experimental.pallas import tpu as pltpu
from jax.sharding import PartitionSpec as P

HEAD_DIM = 128
CAPR = 512
ROWS = 16
ALIGN = 16
CHAINS = 2
NEG = -1e30
SCALE = 1.0 / math.sqrt(HEAD_DIM)
LOG2E = math.log2(math.e)
SPANS = (2, 2, 2, 2)
COPIES = 2


def moves(*arrays):
    return pl.CostEstimate(
        flops=0, bytes_accessed=sum(2 * a.size * a.dtype.itemsize for a in arrays), transcendentals=0
    )


def in_hbm(a):
    return pltpu.with_memory_space_constraint(a, pltpu.HBM)


def my_half():
    return lax.rem(lax.axis_index("ctx"), 2)


def pack_kernel(number, kv, *refs):
    sources, out_ref, sems = refs[:-2], refs[-2], refs[-1]
    block = (1 - my_half()) * kv + number
    copies = []
    at = 0
    for ref in sources[:4]:
        rows = ref.shape[0]
        columns = pl.ds(pl.multiple_of(block * HEAD_DIM, HEAD_DIM), HEAD_DIM)
        copies.append((ref.at[:, columns], out_ref.at[at : at + rows, :]))
        at += rows
    for ref in sources[4:]:
        rows = ref.shape[0]
        heads = (out_ref.shape[0] - at) // rows
        for g in range(heads):
            first = pl.multiple_of((block * heads + g) * HEAD_DIM, HEAD_DIM)
            copies.append((ref.at[:, pl.ds(first, HEAD_DIM)], out_ref.at[at : at + rows, :]))
            at += rows
    copies = [pltpu.make_async_copy(a, b, sems.at[n]) for n, (a, b) in enumerate(copies)]
    for c in copies:
        c.start()
    for c in copies:
        c.wait()


def pack(arrays, queries, kv, number):
    group = queries.shape[1] // arrays[0].shape[1]
    rows = sum(a.shape[0] for a in arrays) + queries.shape[0] * group
    return pl.pallas_call(
        functools.partial(pack_kernel, number, kv),
        in_specs=[pl.BlockSpec(memory_space=pltpu.HBM)] * (len(arrays) + 1),
        out_specs=pl.BlockSpec(memory_space=pltpu.VMEM),
        out_shape=jax.ShapeDtypeStruct((rows, HEAD_DIM), arrays[0].dtype),
        scratch_shapes=[pltpu.SemaphoreType.DMA((len(arrays) + group,))],
        compiler_params=pltpu.CompilerParams(vmem_limit_bytes=4 * 2**20),
        cost_estimate=moves(jax.ShapeDtypeStruct((rows, HEAD_DIM), arrays[0].dtype)),
        name="pack",
    )(*[in_hbm(a) for a in (*arrays, queries)])


def prepare_kernel(kv, *refs):
    sources, q_ref, packed, outs, sems = refs[:4], refs[4], refs[5 : 5 + kv], refs[-3:-1], refs[-1]
    copies = []
    for i in range(kv):
        at = 0
        for ref in sources:
            rows = ref.shape[0]
            first = pl.multiple_of((my_half() * kv + i) * HEAD_DIM, HEAD_DIM)
            copies.append((ref.at[:, pl.ds(first, HEAD_DIM)], packed[i].at[at : at + rows, :]))
            at += rows
    width = outs[0].shape[1]
    for n, out in enumerate(outs):
        columns = pl.ds(pl.multiple_of((my_half() ^ n) * width, width), width)
        copies.append((q_ref.at[:, columns], out))
    copies = [pltpu.make_async_copy(a, b, sems.at[n]) for n, (a, b) in enumerate(copies)]
    for c in copies:
        c.start()
    for c in copies:
        c.wait()


def prepare(arrays, queries, kv):
    rows = sum(a.shape[0] for a in arrays)
    half = jax.ShapeDtypeStruct((queries.shape[0], queries.shape[1] // 2), queries.dtype)
    return pl.pallas_call(
        functools.partial(prepare_kernel, kv),
        in_specs=[pl.BlockSpec(memory_space=pltpu.HBM)] * (len(arrays) + 1),
        out_specs=[pl.BlockSpec(memory_space=pltpu.VMEM)] * (kv + 2),
        out_shape=[jax.ShapeDtypeStruct((rows, HEAD_DIM), queries.dtype)] * kv + [half, half],
        scratch_shapes=[pltpu.SemaphoreType.DMA((4 * kv + 2,))],
        compiler_params=pltpu.CompilerParams(vmem_limit_bytes=2 * 2**20),
        name="prepare",
    )(*[in_hbm(a) for a in (*arrays, queries)])


def attention_kernel(
    key_blocks, query_blocks, number, window, shard_rows, block_rows, near_queries, weight_block,
    new_ref, cache_ref, weight_ref, *rest,
):
    key_blocks, row_blocks = key_blocks(), query_blocks()
    shards = len(key_blocks)
    query_blocks = len(row_blocks)
    reqs = new_ref.shape[1]
    packed = rest[:shards]
    spans = len(SPANS)
    q_refs = rest[shards : -4 - spans]
    out_ref, held = rest[-4 - spans], rest[-3 - spans : -3]
    sorted_q, part, sems = rest[-3:]
    copies = []
    column = 0
    for there in held:
        rows, width = there.shape
        share = rows // COPIES
        for n in range(COPIES):
            first = pl.multiple_of(weight_block() * rows + n * share, ALIGN)
            source = weight_ref.at[pl.ds(first, share), column : column + width]
            target = there.at[n * share : (n + 1) * share, :]
            copies.append(pltpu.make_async_copy(source, target, sems.at[len(copies)]))
            copies[-1].start()
        column += width
    padded = sorted_q.shape[0]
    cols = sorted_q.shape[1]
    group = cols // HEAD_DIM
    all_rows = out_ref.shape[0]

    def new_counts(b, r):
        return new_ref[b, r]

    def cache_counts(b, r):
        return cache_ref[b, r]

    starts = [[jnp.int32(0)] for _ in row_blocks]
    bases = [[] for _ in row_blocks]
    tile_ends = []
    last = jnp.int32(0)
    for r in range(reqs):
        amount = jnp.int32(0)
        for b, block in enumerate(row_blocks):
            bases[b].append(amount)
            amount = amount + new_counts(block, r)
            starts[b].append(starts[b][-1] + new_counts(block, r))
        last = last + (amount + (ROWS - 1)) // ROWS
        tile_ends.append(last)
    tile_starts = [jnp.int32(0)] + tile_ends[:-1]

    offset = lax.broadcasted_iota(jnp.int32, (1, all_rows), 1)
    pos = jnp.zeros((1, all_rows), jnp.int32)
    for b in range(query_blocks):
        here = offset - b * block_rows
        for r in range(reqs):
            mine = (here >= starts[b][r]) & (here < starts[b][r + 1])
            mine = mine & (here >= 0) & (here < block_rows)
            first = tile_starts[r] * ROWS + bases[b][r] - starts[b][r]
            pos = jnp.where(mine, first + here, pos)
    sorter = (lax.broadcasted_iota(jnp.int32, (padded, all_rows), 0) == pos).astype(jnp.bfloat16)
    rows_in = [q[:, number * cols : (number + 1) * cols] for q in q_refs]
    if near_queries:
        first = 2 * (shard_rows + block_rows)
        near = [
            packed[1][first + g * block_rows : first + (g + 1) * block_rows, :]
            for g in range(group)
        ]
        rows_in.insert(1, jnp.concatenate(near, axis=1))
    rows_in = jnp.concatenate(rows_in, axis=0)
    sorted_q[...] = jnp.dot(sorter, rows_in, preferred_element_type=jnp.float32).astype(
        jnp.bfloat16
    )
    part[...] = jnp.zeros_like(part)

    width = shards * (window + block_rows)
    plain = (shards * window) // 128 * 128
    key = lax.broadcasted_iota(jnp.int32, (1, width), 1)
    lane = lax.broadcasted_iota(jnp.int32, (ROWS, 128), 1)
    ones = jnp.ones((width, HEAD_DIM), jnp.bfloat16)

    def tile(i, carry):
        r = jnp.int32(0)
        start_tile = jnp.int32(0)
        for e in tile_ends[:-1]:
            r = r + (i >= e).astype(jnp.int32)
            start_tile = jnp.where(i >= e, e, start_tile)
        inside = None
        key_pos = jnp.full((1, width), -1, jnp.int32)
        ks, vs = [], []
        for j in range(shards):
            shard = key_blocks[j]
            low = jnp.int32(0)
            new_low = jnp.int32(0)
            for o in range(reqs - 1):
                low = low + jnp.where(o < r, cache_counts(shard, o), 0)
                new_low = new_low + jnp.where(o < r, new_counts(shard, o), 0)
            high = low + cache_counts(shard, r)
            new_high = new_low + new_counts(shard, r)
            start = jnp.clip(low // ALIGN * ALIGN, 0, shard_rows - window)
            start = pl.multiple_of(start, ALIGN)
            ks.append(packed[j][pl.ds(start, window), :])
            vs.append(packed[j][pl.ds(pl.multiple_of(start + shard_rows, ALIGN), window), :])
            first = key - j * window + start
            seen = (key >= j * window) & (key < (j + 1) * window)
            seen = seen & (first >= low) & (first < high)
            inside = seen if inside is None else inside | seen
            base = shards * window + j * block_rows
            fresh = key - base
            seen = (key >= base) & (fresh < block_rows)
            key_pos = jnp.where(seen, shard * block_rows + fresh, key_pos)
            inside = inside | (seen & (fresh >= new_low) & (fresh < new_high))
        after = 2 * shard_rows
        for j in range(shards):
            ks.append(packed[j][after : after + block_rows, :])
            vs.append(packed[j][after + block_rows : after + 2 * block_rows, :])
        ks = jnp.concatenate(ks, axis=0)
        vs = jnp.concatenate(vs, axis=0)
        row0 = pl.multiple_of(i * ROWS, ROWS)
        bias = jnp.where(inside, 0.0, NEG)
        t = jnp.zeros((ROWS, 1), jnp.int32)
        among = (i - start_tile) * ROWS + lax.broadcasted_iota(jnp.int32, (ROWS, 1), 0)
        base = jnp.int32(0)
        for block in row_blocks:
            begin = jnp.int32(0)
            for o in range(reqs - 1):
                begin = begin + jnp.where(o < r, new_counts(block, o), 0)
            t = jnp.where(among >= base, block * block_rows + begin + among - base, t)
            base = base + new_counts(block, r)
        causal = jnp.where(key_pos[:, plain:] <= t, bias[:, plain:], NEG)
        values = jnp.concatenate([vs, ones], axis=1)
        logs = jnp.zeros((ROWS, 128), jnp.float32)
        together = group // CHAINS if group % CHAINS == 0 else group
        causal = jnp.concatenate([causal] * together, axis=0)
        for chain in range(0, group, together):
            heads = range(chain, chain + together)
            q = jnp.concatenate(
                [sorted_q[pl.ds(row0, ROWS), g * HEAD_DIM : (g + 1) * HEAD_DIM] for g in heads], axis=0
            )
            scores = lax.dot_general(
                q, ks, (((1,), (1,)), ((), ())), preferred_element_type=jnp.float32
            )
            scores = jnp.concatenate(
                [scores[:, :plain] + bias[:, :plain], scores[:, plain:] + causal], axis=1
            )
            top = jnp.max(scores, axis=1, keepdims=True)
            probs = jnp.exp2((scores - top) * (SCALE * LOG2E)).astype(jnp.bfloat16)
            mixed = jnp.dot(probs, values, preferred_element_type=jnp.float32)
            total = mixed[:, HEAD_DIM:]
            value = (mixed[:, :HEAD_DIM] / total).astype(jnp.bfloat16)
            lse = top * SCALE + jnp.log(total)
            for n, g in enumerate(heads):
                rows = slice(n * ROWS, (n + 1) * ROWS)
                part[pl.ds(row0, ROWS), g * HEAD_DIM : (g + 1) * HEAD_DIM] = value[rows]
                logs = jnp.where(lax.rem(lane, group) == g, lse[rows], logs)
        high = logs.astype(jnp.bfloat16)
        rest_of = logs - high.astype(jnp.float32)
        middle = rest_of.astype(jnp.bfloat16)
        low = rest_of - middle.astype(jnp.float32)
        logs = jnp.where(lane < 2 * group, middle.astype(jnp.float32), low)
        logs = jnp.where(lane < group, high.astype(jnp.float32), logs)
        part[pl.ds(row0, ROWS), cols:] = logs.astype(jnp.bfloat16)
        return carry

    lax.fori_loop(0, last, tile, jnp.int32(0))

    back = (((0,), (0,)), ((), ()))
    out_ref[...] = lax.dot_general(
        sorter, part[...], back, preferred_element_type=jnp.float32
    ).astype(jnp.bfloat16)
    for c in copies:
        c.wait()


def attend(
    counts, packed, queries, cols, number, block_rows, shard_rows, key_blocks, query_blocks, near_queries,
    weight, weight_block,
):
    all_rows = len(query_blocks()) * block_rows
    reqs = counts[0].shape[1]
    padded = (all_rows + reqs * (ROWS - 1)) // ROWS * ROWS
    sets = len(packed)
    window = min(CAPR + ALIGN, shard_rows)
    vmem = pl.BlockSpec(memory_space=pltpu.VMEM)
    return pl.pallas_call(
        functools.partial(
            attention_kernel,
            key_blocks, query_blocks, number, window, shard_rows, block_rows, near_queries, weight_block,
        ),
        in_specs=[pl.BlockSpec(memory_space=pltpu.SMEM)] * 2
        + [pl.BlockSpec(memory_space=pltpu.HBM)]
        + [vmem] * (sets + len(queries)),
        out_specs=[vmem] * (1 + len(SPANS)),
        scratch_shapes=[
            pltpu.VMEM((padded, cols), jnp.bfloat16),
            pltpu.VMEM((padded, cols + 128), jnp.bfloat16),
            pltpu.SemaphoreType.DMA((len(SPANS) * COPIES,)),
        ],
        out_shape=[
            jax.ShapeDtypeStruct((all_rows, cols + 128), jnp.bfloat16),
            *[pltpu.VMEM((cols, weight.shape[1] // 8 * n), weight.dtype) for n in SPANS],
        ],
        compiler_params=pltpu.CompilerParams(vmem_limit_bytes=8 * 2**20),
        cost_estimate=pl.CostEstimate(
            flops=8 * padded * cols * sets * window,
            bytes_accessed=16 * 2**20,
            transcendentals=0,
        ),
        name="attend",
    )(*[in_hbm(c) for c in counts], in_hbm(weight), *packed, *queries)


def log_sums(pieces, group):
    pieces = pieces.astype(jnp.float32)
    return pieces[..., :group] + pieces[..., group : 2 * group] + pieces[..., 2 * group : 3 * group]


def places(dest, out_rows, heads):
    mine = lax.axis_index("head")
    head = lax.div(dest, out_rows)
    if heads & (heads - 1) == 0:
        head = head ^ mine
    else:
        head = lax.rem(head + heads - mine, heads)
    if heads == 4:
        head = jnp.where(head == 1, 2, jnp.where(head == 2, 1, head))
    return head * out_rows + lax.rem(dest, out_rows)


def mixed_head(a_ref, b_ref, g, weights):
    at = slice(g * HEAD_DIM, (g + 1) * HEAD_DIM)
    one = weights[0][:, g : g + 1] * a_ref[:, at].astype(jnp.float32)
    one = one + weights[1][:, g : g + 1] * b_ref[:, at].astype(jnp.float32)
    return one.astype(jnp.bfloat16)


def mixing_weights(a_ref, b_ref, group):
    cols = group * HEAD_DIM
    sa, sb = log_sums(a_ref[:, cols:], group), log_sums(b_ref[:, cols:], group)
    best = jnp.maximum(sa, sb)
    wa, wb = jnp.exp(sa - best), jnp.exp(sb - best)
    whole = wa + wb
    return wa / whole, wb / whole


def mix_kernel(group, a_ref, b_ref, out_ref):
    weights = mixing_weights(a_ref, b_ref, group)
    for g in range(group):
        out_ref[:, g * HEAD_DIM : (g + 1) * HEAD_DIM] = mixed_head(a_ref, b_ref, g, weights)


def mix(a, b):
    vmem = pl.BlockSpec(memory_space=pltpu.VMEM)
    cols = a.shape[1] - 128
    return pl.pallas_call(
        functools.partial(mix_kernel, cols // HEAD_DIM),
        in_specs=[vmem] * 2,
        out_specs=vmem,
        out_shape=jax.ShapeDtypeStruct((a.shape[0], cols), jnp.bfloat16),
        compiler_params=pltpu.CompilerParams(vmem_limit_bytes=4 * 2**20),
        cost_estimate=moves(a, b),
        name="mix",
    )(a, b)


def combine_kernel(group, heads, dest_ref, a_ref, b_ref, far_ref, out_ref, gathered):
    rows = out_ref.shape[0]
    half_rows = a_ref.shape[0]
    block_rows = half_rows // 2
    me = lax.axis_index("ctx")
    weights = mixing_weights(a_ref, b_ref, group)
    dest = places(dest_ref[...].reshape(1, rows), rows // heads, heads)
    landing = (lax.broadcasted_iota(jnp.int32, (rows, rows), 0) == dest).astype(jnp.bfloat16)
    first = [pl.multiple_of((me ^ n) * block_rows, ALIGN) for n in range(4)]
    for g in range(group):
        at = slice(g * HEAD_DIM, (g + 1) * HEAD_DIM)
        one = mixed_head(a_ref, b_ref, g, weights)
        for k in range(2):
            here = slice(k * block_rows, (k + 1) * block_rows)
            gathered[pl.ds(first[k], block_rows), at] = one[here]
            gathered[pl.ds(first[2 + k], block_rows), at] = far_ref[here, at]
    out_ref[...] = jnp.dot(landing, gathered[...], preferred_element_type=jnp.float32).astype(
        jnp.bfloat16
    )


def combine(dest, a, b, far, heads):
    vmem = pl.BlockSpec(memory_space=pltpu.VMEM)
    cols = far.shape[1]
    return pl.pallas_call(
        functools.partial(combine_kernel, cols // HEAD_DIM, heads),
        in_specs=[vmem] * 4,
        out_specs=vmem,
        out_shape=jax.ShapeDtypeStruct((dest.shape[0], cols), jnp.bfloat16),
        scratch_shapes=[pltpu.VMEM((dest.shape[0], cols), jnp.bfloat16)],
        compiler_params=pltpu.CompilerParams(vmem_limit_bytes=6 * 2**20),
        cost_estimate=moves(a, b, far),
        name="combine",
    )(dest, a, b, far)


def project_kernel(parts, added, cuts, step, *refs):
    a_refs, w_refs = refs[:parts], refs[parts : 2 * parts]
    total_refs, outs = refs[2 * parts : 2 * parts + added], refs[2 * parts + added :]

    def columns(j, carry):
        here = pl.ds(pl.multiple_of(j * step, step), step)
        total = total_refs[0][:, here] if added else None
        for a, w in zip(a_refs, w_refs):
            product = jnp.dot(a[...], w[:, here], preferred_element_type=jnp.float32)
            total = product if total is None else total + product
        for (low, high), out in zip(cuts, outs):
            out[:, here] = total[low:high].astype(out.dtype)
        return carry

    lax.fori_loop(0, outs[0].shape[1] // step, columns, 0)


def project(parts, weights, cuts, step, added=()):
    vmem = pl.BlockSpec(memory_space=pltpu.VMEM)
    depth = parts[0].shape[1] * len(parts)
    width = weights[0].shape[1]
    return pl.pallas_call(
        functools.partial(project_kernel, len(parts), len(added), [c[:2] for c in cuts], step),
        in_specs=[vmem] * (2 * len(parts) + len(added)),
        out_specs=[vmem] * len(cuts),
        out_shape=[jax.ShapeDtypeStruct((high - low, width), dtype) for low, high, dtype in cuts],
        compiler_params=pltpu.CompilerParams(vmem_limit_bytes=6 * 2**20),
        cost_estimate=pl.CostEstimate(
            flops=4 * parts[0].shape[0] * depth * width,
            bytes_accessed=depth * width,
            transcendentals=0,
        ),
        name="project",
    )(*parts, *[pltpu.with_memory_space_constraint(w, pltpu.VMEM) for w in weights], *added)


def finish_kernel(counts, *refs):
    out_ref = refs[-1]
    at = n = 0
    for count in counts:
        rows, width = refs[n].shape
        total = refs[n][...]
        for ref in refs[n + 1 : n + count]:
            total = total + ref[:rows, :].astype(jnp.float32)
        out_ref[:, at : at + width] = total.astype(out_ref.dtype)
        at += width
        n += count


def finish(chunks):
    vmem = pl.BlockSpec(memory_space=pltpu.VMEM)
    arrays = [a for chunk in chunks for a in chunk]
    width = sum(chunk[0].shape[1] for chunk in chunks)
    return pl.pallas_call(
        functools.partial(finish_kernel, [len(chunk) for chunk in chunks]),
        in_specs=[vmem] * len(arrays),
        out_specs=vmem,
        out_shape=jax.ShapeDtypeStruct((arrays[0].shape[0], width), jnp.bfloat16),
        compiler_params=pltpu.CompilerParams(vmem_limit_bytes=8 * 2**20),
        name="finish",
    )(*arrays)


def per_device(
    queries,
    cache_keys,
    cache_values,
    new_keys,
    new_values,
    out_weight,
    new_counts,
    cache_counts,
    row_dest,
):
    blocks = lax.axis_size("ctx")
    heads = lax.axis_size("head")
    block_rows = queries.shape[0]
    all_rows = block_rows * blocks
    kv_here = cache_keys.shape[1] // HEAD_DIM
    paired = blocks == 4 and kv_here % 2 == 0
    even = heads & (heads - 1) == 0
    kv = kv_here // 2 if paired else kv_here
    cols = queries.shape[1] // kv_here
    shard_rows = cache_keys.shape[0]
    caches = (cache_keys, cache_values, new_keys, new_values)

    if paired:
        near = [(i, i ^ 1) for i in range(blocks)]
        far = [(i, i ^ 2) for i in range(blocks)]
        across = [(i, i ^ 3) for i in range(blocks)]
        *own_packed, q_mine, q_other = prepare(caches, queries, kv)
        q_far = lax.ppermute(q_mine, "ctx", far)
        q_across = lax.ppermute(q_other, "ctx", across)
        packed = [
            [
                own_packed[i],
                lax.ppermute(pack(caches, queries, kv, i), "ctx", near),
            ]
            for i in range(kv)
        ]
        nearby = lambda ds: lambda: [lax.axis_index("ctx") ^ d for d in ds]
        phases = [
            (nearby((0, 1)), [q_mine], lambda i: lambda: my_half() * kv + i),
            (nearby((2, 3)), [q_far, q_across], lambda i: lambda: (1 - my_half()) * kv + i),
        ]
        key_blocks = nearby((0, 1))
    else:
        rows_in = lax.all_gather(queries, "ctx", axis=0, tiled=True)
        packed = [
            [jnp.concatenate([a[:, i * HEAD_DIM : (i + 1) * HEAD_DIM] for a in caches], axis=0)]
            for i in range(kv)
        ]
        phases = [(lambda: list(range(blocks)), [rows_in], lambda i: lambda: i)]
        key_blocks = lambda: [lax.axis_index("ctx")]

    counts = (new_counts, cache_counts)
    results = [
        attend(
            counts, packed[i], pieces, cols, i, block_rows, shard_rows, key_blocks, query_blocks,
            paired and number == 0, out_weight, weight_block(i),
        )
        for number, (query_blocks, pieces, weight_block) in enumerate(phases)
        for i in range(kv)
    ]
    weights = [r[1:] for r in results]
    results = [r[0] for r in results]
    halving = heads == 4
    out_rows = all_rows // heads

    if paired:
        mine = []
        for i in range(kv):
            own, other = results[i], results[kv + i]
            from_own, from_other = lax.ppermute(own, "ctx", far), lax.ppermute(other, "ctx", far)
            mine.append(combine(row_dest, own, from_other, mix(other, from_own), heads))
        others = [lax.ppermute(a, "ctx", near) for a in mine]
    else:
        mine, others = [], []
        group = cols // HEAD_DIM
        landing = jnp.arange(all_rows)[:, None] == places(row_dest, out_rows, heads)[None, :]
        for part in results:
            got = lax.all_to_all(
                part.reshape(blocks, block_rows, cols + 128), "ctx", 0, 0, tiled=True
            ).reshape(blocks, block_rows, cols + 128)
            logs = log_sums(got[..., cols:], group)
            share = jnp.exp(logs - jnp.max(logs, axis=0)[None])
            share = share / jnp.sum(share, axis=0)[None]
            stacked = got[..., :cols].reshape(blocks, block_rows, group, HEAD_DIM)
            one = jnp.sum(share[..., None] * stacked.astype(jnp.float32), axis=0)
            one = one.astype(jnp.bfloat16).reshape(block_rows, cols)
            one = lax.all_gather(one, "ctx", axis=0, tiled=True)
            mine.append(
                jnp.dot(landing.astype(one.dtype), one, preferred_element_type=jnp.float32).astype(
                    one.dtype
                )
            )

    hops = [[(i, i ^ d if even else (i + d) % heads) for i in range(heads)] for d in range(heads)]
    step = out_weight.shape[1] // 8
    direct_cuts = [
        (d * out_rows, (d + 1) * out_rows, jnp.bfloat16 if d else jnp.float32) for d in range(heads)
    ]
    pair_cuts = [
        (0, out_rows, jnp.float32),
        (out_rows, 2 * out_rows, jnp.float32),
        (2 * out_rows, 4 * out_rows, jnp.bfloat16),
    ]
    chunks = []
    for number in range(len(SPANS)):
        span = [w[number] for w in weights]
        by_pairs = halving
        cuts = pair_cuts if by_pairs else direct_cuts
        if others and number == len(SPANS) - 1:
            whole = [(0, all_rows, jnp.float32)]
            begun = project(mine, span[:kv], whole, step)
            shares = project(others, span[kv:], cuts, step, begun)
        elif others:
            shares = project(mine + others, span, cuts, step)
        else:
            shares = project(mine, span, cuts, step)
        if by_pairs:
            got = lax.ppermute(shares[2], "head", hops[1])
            away = (shares[1] + got[out_rows:].astype(jnp.float32)).astype(jnp.bfloat16)
            chunks.append([shares[0], got, lax.ppermute(away, "head", hops[2])])
        else:
            if halving:
                shares = [shares[i] for i in (0, 2, 1, 3)]
            chunks.append(
                [shares[0]] + [lax.ppermute(shares[d], "head", hops[d]) for d in range(1, heads)]
            )
    return finish(chunks)


def solution(mesh):
    return jax.shard_map(
        per_device,
        mesh=mesh,
        in_specs=(
            P(("groups", "ctx"), "head"),
            P(("groups", "ctx"), "head"),
            P(("groups", "ctx"), "head"),
            P(("groups", "ctx"), "head"),
            P(("groups", "ctx"), "head"),
            P("head", "ctx"),
            P("groups", None),
            P("groups", None),
            P("groups"),
        ),
        out_specs=P(("groups", "head"), "ctx"),
        check_vma=False,
    )
```
